256 devices in a mesh: dp: 8 (over y, x_hi), tok: 8 (over z), hid: 4 (over x_lo, core).
Axes of the slice: x: 4 (x_hi: 2, x_lo: 2; x = x_hi * 2 + x_lo), y: 4, z: 8, core: 2. Of those that a mesh axis runs over, the one named last changes fastest.
Arguments:
- tokens: bfloat16 [8192, 3072], P(('dp', 'tok'), 'hid'), may hold values from -40 to 40
- w_in: bfloat16 [3072, 12288], P('hid', 'tok'), may hold values from -0.108253175 to 0.108253175
- w_out: bfloat16 [12288, 3072], P('tok', 'hid'), may hold values from -0.0546875 to 0.0546875
- gain: float32 [3072], P('hid'), may hold values from 0.2 to 4, as said below
- cotangent: bfloat16 [8192, 3072], P(('dp', 'tok'), 'hid'), may hold values from -6 to 6
Outputs:
- mixed: bfloat16 [8192, 3072], P(('dp', 'tok'), 'hid')
- grad_input: bfloat16 [8192, 3072], P(('dp', 'tok'), 'hid')
- grad_w_in: bfloat16 [3072, 12288], P('hid', 'tok')
- grad_w_out: bfloat16 [12288, 3072], P('tok', 'hid')
The draws below stay inside these ranges and needn't reach their ends.
Inputs may be any that keep to these rules, and one draw needn't show every extreme that they name: `gain`: positive.
All inputs are finite; a program needn't handle non-finite values.
Results may differ from the reference program's by a relative error of at most 0.024.
Values may be sent and summed in bfloat16 or wider, within the bound.
A program may use at most 128 MiB of HBM per device.

```python
import math
import jax
import jax.numpy as jnp
from jax import lax

D = 3072
FF = 12288
TOK_DEV = 128
TOKENS = 8192
N_DP = 8
N_TOK = 8
N_HID = 4


def draw_tokens(key, part):
    base_key = jax.random.fold_in(key, 11)
    key_base, key_col, key_row = jax.random.split(base_key, 3)
    trend = jnp.exp(math.log(3.0) * jnp.arange(D, dtype=jnp.float32) / D)
    col_scale = trend * jnp.exp(jax.random.uniform(key_col, (D,), jnp.float32) * math.log(3.3)) / 3.0
    row_scale = 0.3 * jnp.exp(jax.random.uniform(key_row, (TOKENS, 1), jnp.float32) * math.log(10.0))
    values = jnp.clip(jax.random.normal(key_base, (TOKENS, D), jnp.float32), -4.0, 4.0)
    return (values * col_scale[None, :] * row_scale).astype(jnp.bfloat16)


def draw_w_in(key, part):
    key = jax.random.fold_in(key, 23)
    key_noise, key_shared = jax.random.split(key, 2)
    noise = jnp.clip(jax.random.normal(key_noise, (D, FF), jnp.float32), -4.0, 4.0)
    shared = 0.5 * jnp.clip(jax.random.normal(key_shared, (1, FF), jnp.float32), -2.5, 2.5)
    return ((noise + shared) * (1.0 / math.sqrt(D))).astype(jnp.bfloat16)


def draw_gain(key, part):
    key = jax.random.fold_in(key, 37)
    position = jnp.arange(D, dtype=jnp.float32) / (D - 1)
    rise_log = math.log(4.0)
    slope = jnp.exp(rise_log * (position - 0.5))
    rough = jax.random.uniform(key, (D,), jnp.float32, 0.7, 1.3)
    return (slope * rough).astype(jnp.float32)


def block_scale(stream_key, dims, cuts, smallest, largest):
    loudness = 1.0
    for dim, shards_of in cuts:
        steps = jax.random.uniform(jax.random.fold_in(jax.random.fold_in(stream_key, 6), dim), (shards_of,), jnp.float32, smallest / len(cuts), largest / len(cuts))
        loudness = loudness * jnp.repeat(jnp.exp(steps), dims[dim] // shards_of).reshape((-1,) + (1,) * (len(dims) - 1 - dim))
    return loudness


def gaussian(key, extent, width, reach, cuts=(), held_as=jnp.bfloat16):
    array = width * jax.random.normal(key, extent, jnp.float32)
    if cuts:
        array = array * block_scale(key, extent, cuts, -0.22, 0.18)
    return jnp.clip(array, -reach, reach).astype(held_as)


def setup_inputs(seed: int = 0) -> dict:
    splits = jax.random.split(jax.random.key(seed), 6)
    return {
        "tokens": draw_tokens(jax.random.fold_in(splits[5], 71), 0),
        "w_in": draw_w_in(jax.random.fold_in(splits[5], 71), 0),
        "w_out": gaussian(splits[2], (FF, D), FF ** -0.5, 0.0546875, ((0, 8), (1, 4))),
        "gain": draw_gain(jax.random.fold_in(splits[5], 71), 0),
        "cotangent": gaussian(splits[4], (TOKENS, D), 1.0, 6.0, ((0, 64), (1, 4))),
    }


norm_eps = 1e-06

def gelu_pair(pre_act):
    cdf_part = 0.5 * (1.0 + jax.scipy.special.erf(pre_act * (1.0 / math.sqrt(2.0))))
    dens_part = jnp.exp(-0.5 * pre_act * pre_act) * (1.0 / math.sqrt(2.0 * math.pi))
    return (pre_act * cdf_part, cdf_part + pre_act * dens_part)

def blocked_sum(left_op, right_op, n_parts):
    part_width = left_op.shape[1] // n_parts
    running = jnp.zeros((left_op.shape[0], right_op.shape[1]), jnp.float32)
    for index in range(n_parts):
        partial_value = jnp.dot(left_op[:, index * part_width:(index + 1) * part_width], right_op[index * part_width:(index + 1) * part_width], preferred_element_type=jnp.float32)
        rounded = lax.optimization_barrier(partial_value.astype(jnp.bfloat16))
        running = running + rounded.astype(jnp.float32)
    return running

def reference(tokens, w_in, w_out, gain, cotangent):
    group_rows = TOK_DEV * N_TOK
    grad_scale = 1.0 / math.sqrt(TOKENS)
    w_out_t = w_out.T
    w_in_t = w_in.T

    def group_step(grad_sums, inputs):
        tok_block, cot_block = inputs
        tok_float = tok_block.astype(jnp.float32)
        row_mean = lax.optimization_barrier(jnp.mean(tok_float, axis=1, keepdims=True))
        row_var = lax.optimization_barrier(jnp.mean(tok_float * tok_float, axis=1, keepdims=True)) - row_mean * row_mean
        row_rstd = lax.rsqrt(row_var + norm_eps)
        centred = (tok_float - row_mean) * row_rstd
        normed = (centred * gain[None, :]).astype(jnp.bfloat16)
        pre_act = blocked_sum(normed, w_in, N_HID)
        act_whole, slopes = gelu_pair(pre_act)
        hidden = act_whole.astype(jnp.bfloat16)
        branch = blocked_sum(hidden, w_out, N_TOK)
        mixed = (tok_float + branch).astype(jnp.bfloat16)
        grad_act = blocked_sum(cot_block, w_out_t, N_HID)
        grad_hidden = (grad_act * slopes).astype(jnp.bfloat16)
        grad_normed = blocked_sum(grad_hidden, w_in_t, N_TOK)
        grad_scaled = grad_normed * gain[None, :]
        first_mean = lax.optimization_barrier(jnp.mean(grad_scaled, axis=1, keepdims=True))
        second_mean = lax.optimization_barrier(jnp.mean(grad_scaled * centred, axis=1, keepdims=True))
        grad_input = (cot_block.astype(jnp.float32) + row_rstd * (grad_scaled - first_mean - centred * second_mean)).astype(jnp.bfloat16)
        in_part = (jnp.dot(normed.T, grad_hidden, preferred_element_type=jnp.float32) * grad_scale).astype(jnp.bfloat16)
        out_part = (jnp.dot(hidden.T, cot_block, preferred_element_type=jnp.float32) * grad_scale).astype(jnp.bfloat16)
        new_sums = (grad_sums[0] + in_part.astype(jnp.float32), grad_sums[1] + out_part.astype(jnp.float32))
        return (new_sums, (mixed, grad_input))
    init_sums = (jnp.zeros((D, FF), jnp.float32), jnp.zeros((FF, D), jnp.float32))
    grad_sums, outputs = lax.scan(group_step, init_sums, (tokens.reshape(N_DP, group_rows, D), cotangent.reshape(N_DP, group_rows, D)))
    mixed = outputs[0].reshape(TOKENS, D)
    grad_input = outputs[1].reshape(TOKENS, D)
    return (mixed, grad_input, grad_sums[0].astype(jnp.bfloat16), grad_sums[1].astype(jnp.bfloat16))
```

```python
import functools
import math

import jax
import jax.numpy as jnp
from jax import lax
from jax.experimental import pallas as pl
from jax.experimental.pallas import tpu as pltpu
from jax.sharding import PartitionSpec as P

D = 3072
ROWS = 128
WIDTH = 768
TOK = 1024
N_TOK = 8
N_Y = 4
QUARTER = WIDTH // N_Y
EIGHTH = QUARTER // 2
SHARE = ROWS // 2
PIECES = 4
MAX_COPIES = 200

norm_eps = 1e-06
GRAD_SCALE = 1.0 / math.sqrt(8192)
MESH = pl.DeviceIdType.MESH
BF16 = jnp.bfloat16
F32 = jnp.float32


def gelu_pair(pre_act):
    cdf_part = 0.5 * (1.0 + lax.erf(pre_act * (1.0 / math.sqrt(2.0))))
    dens_part = jnp.exp(-0.5 * pre_act * pre_act) * (1.0 / math.sqrt(2.0 * math.pi))
    return (pre_act * cdf_part, cdf_part + pre_act * dens_part)


def dot(left_op, right_op):
    return jnp.dot(left_op, right_op, preferred_element_type=F32)


def right_contract(left_op, right_op):
    return lax.dot_general(
        left_op, right_op, (((1,), (1,)), ((), ())), preferred_element_type=F32
    )


def row_contract(left_op, right_op):
    return lax.dot_general(
        left_op, right_op, (((0,), (0,)), ((), ())), preferred_element_type=F32
    )


def block(start, size):
    return pl.ds(start if isinstance(start, int) else pl.multiple_of(start, 16), size)


def kernel(
    tok_ref, win_ref, wout_ref, gain_ref, cot_ref,
    mixed_ref, gin_ref, gwin_ref, gwout_ref,
    winc, woutc, xf, cf, pf, rf, pb, rb, slopes, hid, ghid,
    branch, zf, gnorm, zb, stat_out, stat_in, totals, scaled,
    dw, anti, near, qsum, far, ssem, rsem, lsem,
):
    dp, z, h = lax.axis_index("dp"), lax.axis_index("tok"), lax.axis_index("hid")
    y, xh = dp // 2, dp % 2
    xl, c = h // 2, h % 2
    zp, zm = (dp, (z + 1) % N_TOK, h), (dp, (z + N_TOK - 1) % N_TOK, h)
    sib = (dp, z, xl * 2 + 1 - c)
    xn = (dp, z, (1 - xl) * 2 + c)
    diag = (dp, z, (1 - xl) * 2 + 1 - c)
    yp, ym = (((y + 1) % N_Y) * 2 + xh, z, h), (((y + N_Y - 1) % N_Y) * 2 + xh, z, h)
    xo = (y * 2 + 1 - xh, z, h)
    peers = (zp, zm, sib, xn, diag, yp, ym, xo)

    barrier = pltpu.get_barrier_semaphore()
    for peer in peers:
        pl.semaphore_signal(barrier, inc=1, device_id=peer, device_id_type=MESH)
    pl.semaphore_wait(barrier, len(peers))

    sent = []

    def send(src, dst, peer):
        i = len(sent)
        copy = pltpu.make_async_remote_copy(
            src_ref=src, dst_ref=dst, send_sem=ssem.at[i], recv_sem=rsem.at[i],
            device_id=peer, device_id_type=MESH,
        )
        copy.start()
        sent.append(copy)
        return copy

    own_half, sib_half = c * WIDTH, (1 - c) * WIDTH
    lane_own = pl.ds(pl.multiple_of(own_half, WIDTH), WIDTH)
    lane_sib = pl.ds(pl.multiple_of(sib_half, WIDTH), WIDTH)
    local = [
        pltpu.make_async_copy(wout_ref.at[lane_own, :], woutc.at[c], lsem.at[0]),
        pltpu.make_async_copy(win_ref.at[:, lane_own], winc.at[c], lsem.at[1]),
        pltpu.make_async_copy(cot_ref, cf.at[c, block(0, ROWS)], lsem.at[2]),
    ]
    for copy in local:
        copy.start()

    def slot(r, lo=0, size=ROWS):
        return block(r * ROWS + lo, size)

    def ring_first(src, buf):
        return [
            (send(src, buf.at[c, slot(1)], zp),),
            (send(src, buf.at[c, slot(2)], zm),),
            send(src, buf.at[c, slot(0)], sib),
        ]

    ring = {"c": {}, "x": {}}
    sib_copies = {"c": {}, "x": {}}
    bufs = {"c": cf, "x": xf}

    def start_ring(name, src):
        up, down, across = ring_first(src, bufs[name])
        ring[name][1] = up + down
        sib_copies[name][0] = across

    def ring_wait(name, k):
        buf = bufs[name]
        for copy in ring[name][k]:
            copy.wait_recv()
        for r in (2 * k - 1, 2 * k) if k < 4 else (7,):
            sib_copies[name][r] = send(buf.at[c, slot(r)], buf.at[c, slot(r)], sib)

    def ring_forward(name, k):
        buf = bufs[name]
        a, b = 2 * k - 1, 2 * k
        if k < 3:
            ring[name][k + 1] = (
                send(buf.at[c, slot(a)], buf.at[c, slot(a + 2)], zp),
                send(buf.at[c, slot(b)], buf.at[c, slot(b + 2)], zm),
            )
        else:
            lo, hi = (0, SHARE), (SHARE, SHARE)
            ring[name][4] = (
                send(buf.at[c, slot(a, *lo)], buf.at[c, slot(7, *lo)], zp),
                send(buf.at[c, slot(b, *hi)], buf.at[c, slot(7, *hi)], zm),
            )

    start_ring("c", cot_ref)
    weight_copies = [
        send(wout_ref.at[lane_sib, :], woutc.at[c], sib),
        send(win_ref.at[:, lane_sib], winc.at[c], sib),
    ]

    lanes = lax.broadcasted_iota(jnp.int32, (ROWS, ROWS), 1)

    def share_stats(i, first, second):
        stat_out[i] = jnp.where(lanes == 0, first, second).T[0:8]
        return [
            send(stat_out.at[i], stat_in.at[i, j], peer)
            for j, peer in enumerate((xn, diag, sib))
        ]

    def total_stats(i, copies):
        for copy in copies:
            copy.wait_recv()
        total = (stat_out[i] + stat_in[i, 2]) + (stat_in[i, 0] + stat_in[i, 1])
        columns = jnp.concatenate([total] * (ROWS // 8), axis=0).T
        return columns[:, 0:1], columns[:, 1:2]

    tok_float = tok_ref[...].astype(F32)
    stats = share_stats(
        0,
        jnp.sum(tok_float, axis=1, keepdims=True),
        jnp.sum(tok_float * tok_float, axis=1, keepdims=True),
    )

    def partial_product(src, weights, dst, r, transposed):
        rows = slot(r)

        def tile(n, carry):
            cols = pl.ds(pl.multiple_of(n * 256, 256), 256)
            if transposed:
                total = right_contract(src[0, rows], weights[0, cols, :])
                total += right_contract(src[1, rows], weights[1, cols, :])
            else:
                total = dot(src[0, rows], weights[0, :, cols])
                total += dot(src[1, rows], weights[1, :, cols])
            dst[rows, cols] = total.astype(BF16)
            return carry

        lax.fori_loop(0, 3, tile, 0)

    partial_copies = {"f": {}, "b": {}}

    def send_partial(name, part, landing, r):
        partial_copies[name][r] = send(
            part.at[block(r * ROWS + (1 - xl) * SHARE, SHARE)],
            landing.at[block(r * SHARE, SHARE)],
            xn,
        )

    def f1(r):
        sib_copies["x"][r].wait_recv()
        partial_product(xf, winc, pf, r, False)
        send_partial("f", pf, rf, r)

    def b1(r):
        sib_copies["c"][r].wait_recv()
        partial_product(cf, woutc, pb, r, True)
        send_partial("b", pb, rb, r)

    share_copies = {"f": {}, "b": {}}
    whole_copies = {"f": {}, "b": {}}

    def send_share(name, buf, r):
        mine = buf.at[c, block(r * ROWS + xl * SHARE, SHARE)]
        share_copies[name][r] = send(mine, mine, xn)

    def f2(r):
        partial_copies["f"][r].wait_recv()

        def tile(n, carry):
            k = n * 16
            pre_act = pf[block(r * ROWS + xl * SHARE + k, 16), :].astype(F32)
            pre_act += rf[block(r * SHARE + k, 16), :].astype(F32)
            act, slope = gelu_pair(pre_act)
            slopes[block(r * SHARE + k, 16), :] = slope
            hid[c, block(r * ROWS + xl * SHARE + k, 16), :] = act.astype(BF16)
            return carry

        lax.fori_loop(0, SHARE // 16, tile, 0)
        send_share("f", hid, r)

    def b2(r):
        partial_copies["b"][r].wait_recv()

        def tile(n, carry):
            k = n * 16
            grad = pb[block(r * ROWS + xl * SHARE + k, 16), :].astype(F32)
            grad += rb[block(r * SHARE + k, 16), :].astype(F32)
            grad *= slopes[block(r * SHARE + k, 16), :]
            ghid[c, block(r * ROWS + xl * SHARE + k, 16), :] = grad.astype(BF16)
            return carry

        lax.fori_loop(0, SHARE // 16, tile, 0)
        send_share("b", ghid, r)

    def third(name, buf, r):
        share_copies[name][r].wait_recv()
        whole = buf.at[c, slot(r)]
        whole_copies[name][r] = send(whole, whole, sib)

    def f3(r):
        third("f", hid, r)

    def b3(r):
        third("b", ghid, r)

    def whole_wait(name):
        for r in range(N_TOK):
            whole_copies[name][r].wait_recv()

    def product_rows(src, dst, i, transposed):
        rows = block(i * 256, 256)

        def tile(n, carry):
            cols = pl.ds(pl.multiple_of(n * 256, 256), 256)
            if transposed:
                total = right_contract(src[0, rows], win_ref[cols, 0:WIDTH])
                total += right_contract(src[1, rows], win_ref[cols, WIDTH : 2 * WIDTH])
            else:
                total = dot(src[0, rows], wout_ref[0:WIDTH, cols])
                total += dot(src[1, rows], wout_ref[WIDTH : 2 * WIDTH, cols])
            dst[rows, cols] = total.astype(BF16)
            return carry

        lax.fori_loop(0, 3, tile, 0)

    def add_rows(dst, at, src, rows, count):
        def tile(n, carry):
            here = block(at + n * 16, 16)
            there = block(rows + n * 16, 16)
            dst[here, :] = (dst[here, :].astype(F32) + src[there, :].astype(F32)).astype(BF16)
            return carry

        lax.fori_loop(0, count // 16, tile, 0)

    back = {"f": {}, "b": {}}

    def ring_back(name, part, landing, k):
        if k == 4:
            back[name][4] = (
                send(part.at[slot(7, 0, SHARE)], landing.at[slot(5, 0, SHARE)], zm),
                send(part.at[slot(7, SHARE, SHARE)], landing.at[slot(6, SHARE, SHARE)], zp),
            )
            return
        a, b = 2 * k - 1, 2 * k
        for copy in back[name][k + 1]:
            copy.wait_recv()
        if k == 3:
            add_rows(part, a * ROWS, landing, a * ROWS, SHARE)
            add_rows(part, b * ROWS + SHARE, landing, b * ROWS + SHARE, SHARE)
        else:
            add_rows(part, a * ROWS, landing, a * ROWS, ROWS)
            add_rows(part, b * ROWS, landing, b * ROWS, ROWS)
        to_a, to_b = (0, 7) if k == 1 else (a - 2, b - 2)
        back[name][k] = (
            send(part.at[slot(a)], landing.at[slot(to_a)], zm),
            send(part.at[slot(b)], landing.at[slot(to_b)], zp),
        )

    def ring_total(name, part, landing):
        for copy in back[name][1]:
            copy.wait_recv()
        total = part[slot(0), :].astype(F32) + landing[slot(0), :].astype(F32)
        return total + landing[slot(7), :].astype(F32)

    qa, qb, qo = (y + 1) % N_Y, (y + N_Y - 1) % N_Y, (y + 2) % N_Y

    def weight_product(p):
        def tile(n, carry):
            cols = pl.ds(pl.multiple_of(n * 256, 256), 256)
            if p < 2:
                total = row_contract(hid[p, :, cols], cf[c])
            else:
                total = row_contract(xf[c, :, cols], ghid[p - 2])
            dw[p, cols, :] = (total * GRAD_SCALE).astype(BF16)
            return carry

        lax.fori_loop(0, 3, tile, 0)

    first_hop, second_hop, far_copies, spread, spread_on = {}, {}, {}, {}, {}
    low, high = block(0, EIGHTH), block(EIGHTH, EIGHTH)

    def r1(p):
        part = dw.at[p]
        first_hop[p] = (
            send(part.at[block(qo * QUARTER, EIGHTH)], anti.at[p, low], yp),
            send(part.at[block(qo * QUARTER + EIGHTH, EIGHTH)], anti.at[p, high], ym),
        )
        second_hop[p] = (
            send(part.at[block(qa * QUARTER + EIGHTH, EIGHTH)], near.at[p, 0, high], yp),
            send(part.at[block(qb * QUARTER, EIGHTH)], near.at[p, 1, low], ym),
        )

    def r2(p):
        part = dw.at[p]
        for copy in first_hop[p]:
            copy.wait_recv()
        add_rows(part, qa * QUARTER, anti.at[p], 0, EIGHTH)
        add_rows(part, qb * QUARTER + EIGHTH, anti.at[p], EIGHTH, EIGHTH)
        second_hop[p] += (
            send(part.at[block(qa * QUARTER, EIGHTH)], near.at[p, 0, low], yp),
            send(part.at[block(qb * QUARTER + EIGHTH, EIGHTH)], near.at[p, 1, high], ym),
        )

    def r3(p):
        for copy in second_hop[p]:
            copy.wait_recv()

        def tile(n, carry):
            rows = block(n * 16, 16)
            total = dw[p, block(y * QUARTER + n * 16, 16), :].astype(F32)
            total += near[p, 0, rows, :].astype(F32) + near[p, 1, rows, :].astype(F32)
            qsum[p, rows, :] = total.astype(BF16)
            return carry

        lax.fori_loop(0, QUARTER // 16, tile, 0)
        far_copies[p] = send(qsum.at[p], far.at[p], xo)

    def out_rows(p, start, size):
        if p < 2:
            return gwout_ref, (block(p * WIDTH + start, size), slice(None))
        return gwin_ref, (block(start, size), pl.ds((p - 2) * WIDTH, WIDTH))

    def out_at(p, start, size):
        ref, where = out_rows(p, start, size)
        return ref.at[where]

    def r4(p):
        far_copies[p].wait_recv()

        def tile(n, carry):
            rows = block(n * 16, 16)
            total = qsum[p, rows, :].astype(F32) + far[p, rows, :].astype(F32)
            ref, where = out_rows(p, y * QUARTER + n * 16, 16)
            ref[where] = total.astype(BF16)
            return carry

        lax.fori_loop(0, QUARTER // 16, tile, 0)
        own = out_at(p, y * QUARTER, QUARTER)
        spread[p] = (send(own, own, yp), send(own, own, ym))

    def r5(p):
        for copy in spread[p]:
            copy.wait_recv()
        behind = out_at(p, qb * QUARTER, EIGHTH)
        ahead = out_at(p, qa * QUARTER + EIGHTH, EIGHTH)
        spread_on[p] = (send(behind, behind, yp), send(ahead, ahead, ym))

    def r6(p):
        for copy in spread_on[p]:
            copy.wait_recv()

    local[0].wait()
    local[2].wait()
    weight_copies[0].wait_recv()
    b1(0)
    row_sum, square_sum = total_stats(0, stats)
    row_mean = row_sum / D
    row_rstd = lax.rsqrt(square_sum / D - row_mean * row_mean + norm_eps)
    totals[...] = jnp.where(lanes == 0, row_mean, row_rstd)
    centred = (tok_float - row_mean) * row_rstd
    xf[c, slot(0)] = (centred * gain_ref[...]).astype(BF16)
    start_ring("x", xf.at[c, slot(0)])
    local[1].wait()
    weight_copies[1].wait_recv()
    f1(0)
    ring_wait("c", 1)
    b1(1), b1(2)
    ring_wait("x", 1), ring_forward("x", 1)
    f1(1), f1(2), f2(0)
    ring_wait("x", 2), ring_forward("x", 2), ring_forward("c", 1)
    f1(3), f1(4), f2(1), f2(2), f3(0)
    ring_wait("x", 3), ring_forward("x", 3)
    f1(5), f1(6), f2(3), f2(4), f3(1), f3(2)
    ring_wait("c", 2), ring_forward("c", 2)
    ring_wait("x", 4)
    f1(7), f2(5), f2(6), f3(3), f3(4)
    b1(3), b1(4)
    f2(7)
    ring_wait("c", 3), ring_forward("c", 3)
    f3(5), f3(6)
    b1(5), b1(6)
    f3(7)
    b2(0), b2(1), b2(2)
    ring_wait("c", 4)
    b1(7)
    whole_wait("f")
    weight_product(0), r1(0)
    weight_product(1), r1(1)
    b2(3), b2(4), b3(0), b3(1), b3(2)
    product_rows(hid, branch, 3, False), ring_back("f", branch, zf, 4)
    r2(0), r2(1)
    b2(5), b2(6), b3(3), b3(4)
    product_rows(hid, branch, 2, False), ring_back("f", branch, zf, 3)
    r3(0), b2(7), b3(5), b3(6)
    product_rows(hid, branch, 1, False), ring_back("f", branch, zf, 2)
    r3(1), r4(0), b3(7)
    product_rows(hid, branch, 0, False), ring_back("f", branch, zf, 1)
    r4(1)
    whole_wait("b")
    weight_product(2), r1(2)
    weight_product(3), r1(3)
    product_rows(ghid, gnorm, 3, True), ring_back("b", gnorm, zb, 4)
    r5(0), r2(2)
    r5(1), r2(3)
    product_rows(ghid, gnorm, 2, True), ring_back("b", gnorm, zb, 3)
    mixed_ref[...] = (
        tok_ref[...].astype(F32) + ring_total("f", branch, zf)
    ).astype(BF16)
    product_rows(ghid, gnorm, 1, True), ring_back("b", gnorm, zb, 2)
    r3(2)
    product_rows(ghid, gnorm, 0, True), ring_back("b", gnorm, zb, 1)
    r3(3), r4(2)

    grad_scaled = ring_total("b", gnorm, zb) * gain_ref[...]
    scaled[...] = grad_scaled
    row_mean, row_rstd = totals[:, 0:1], totals[:, 1:2]
    centred = (tok_ref[...].astype(F32) - row_mean) * row_rstd
    stats = share_stats(
        1,
        jnp.sum(grad_scaled, axis=1, keepdims=True),
        jnp.sum(grad_scaled * centred, axis=1, keepdims=True),
    )
    r4(3)
    r5(2)
    first_sum, second_sum = total_stats(1, stats)
    gin_ref[...] = (
        cot_ref[...].astype(F32)
        + row_rstd * (scaled[...] - first_sum / D - centred * (second_sum / D))
    ).astype(BF16)
    r5(3)
    for p in range(PIECES):
        r6(p)
    for copy in sent:
        copy.wait_send()


def shards(tokens, w_in, w_out, gain, cotangent):
    vmem = pl.BlockSpec(memory_space=pltpu.VMEM)
    return pl.pallas_call(
        kernel,
        out_shape=(
            jax.ShapeDtypeStruct((ROWS, WIDTH), BF16),
            jax.ShapeDtypeStruct((ROWS, WIDTH), BF16),
            jax.ShapeDtypeStruct((WIDTH, 2 * WIDTH), BF16),
            jax.ShapeDtypeStruct((2 * WIDTH, WIDTH), BF16),
        ),
        in_specs=[vmem] * 5,
        out_specs=(vmem,) * 4,
        scratch_shapes=[
            pltpu.VMEM((2, WIDTH, WIDTH), BF16),
            pltpu.VMEM((2, WIDTH, WIDTH), BF16),
            pltpu.VMEM((2, TOK, WIDTH), BF16),
            pltpu.VMEM((2, TOK, WIDTH), BF16),
            pltpu.VMEM((TOK, WIDTH), BF16),
            pltpu.VMEM((TOK // 2, WIDTH), BF16),
            pltpu.VMEM((TOK, WIDTH), BF16),
            pltpu.VMEM((TOK // 2, WIDTH), BF16),
            pltpu.VMEM((TOK // 2, WIDTH), F32),
            pltpu.VMEM((2, TOK, WIDTH), BF16),
            pltpu.VMEM((2, TOK, WIDTH), BF16),
            pltpu.VMEM((TOK, WIDTH), BF16),
            pltpu.VMEM((TOK, WIDTH), BF16),
            pltpu.VMEM((TOK, WIDTH), BF16),
            pltpu.VMEM((TOK, WIDTH), BF16),
            pltpu.VMEM((2, 8, ROWS), F32),
            pltpu.VMEM((2, 3, 8, ROWS), F32),
            pltpu.VMEM((ROWS, ROWS), F32),
            pltpu.VMEM((ROWS, WIDTH), F32),
            pltpu.VMEM((PIECES, WIDTH, WIDTH), BF16),
            pltpu.VMEM((PIECES, QUARTER, WIDTH), BF16),
            pltpu.VMEM((PIECES, 2, QUARTER, WIDTH), BF16),
            pltpu.VMEM((PIECES, QUARTER, WIDTH), BF16),
            pltpu.VMEM((PIECES, QUARTER, WIDTH), BF16),
            pltpu.SemaphoreType.DMA((MAX_COPIES,)),
            pltpu.SemaphoreType.DMA((MAX_COPIES,)),
            pltpu.SemaphoreType.DMA((3,)),
        ],
        compiler_params=pltpu.CompilerParams(
            collective_id=0, has_side_effects=True, vmem_limit_bytes=60 << 20
        ),
        cost_estimate=pl.CostEstimate(
            flops=6 * 2 * TOK * WIDTH * 2 * WIDTH, bytes_accessed=12 << 20, transcendentals=0
        ),
        name="mlp_block",
    )(tokens, w_in, w_out, gain.reshape(1, WIDTH), cotangent)


def solution(mesh):
    in_specs = (
        P(("dp", "tok"), "hid"),
        P("hid", "tok"),
        P("tok", "hid"),
        P("hid"),
        P(("dp", "tok"), "hid"),
    )
    out_specs = (P(("dp", "tok"), "hid"), P(("dp", "tok"), "hid"), P("hid", "tok"), P("tok", "hid"))
    return jax.shard_map(shards, mesh=mesh, in_specs=in_specs, out_specs=out_specs, check_vma=False)
```

```python
import functools
import math

import jax
import jax.numpy as jnp
from jax import lax
from jax.experimental import pallas as pl
from jax.experimental.pallas import tpu as pltpu
from jax.sharding import PartitionSpec as P

D = 3072
ROWS = 128
WIDTH = 768
TOK = 1024
N_TOK = 8
N_Y = 4
QUARTER = WIDTH // N_Y
EIGHTH = QUARTER // 2
SHARE = ROWS // 2
PIECES = 4
X_LAST = (1, 2)
MAX_COPIES = 200

norm_eps = 1e-06
GRAD_SCALE = 1.0 / math.sqrt(8192)
MESH = pl.DeviceIdType.MESH
BF16 = jnp.bfloat16
F32 = jnp.float32


def gelu_pair(pre_act):
    cdf_part = 0.5 * (1.0 + lax.erf(pre_act * (1.0 / math.sqrt(2.0))))
    dens_part = jnp.exp(-0.5 * pre_act * pre_act) * (1.0 / math.sqrt(2.0 * math.pi))
    return (pre_act * cdf_part, cdf_part + pre_act * dens_part)


def dot(left_op, right_op):
    return jnp.dot(left_op, right_op, preferred_element_type=F32)


def right_contract(left_op, right_op):
    return lax.dot_general(
        left_op, right_op, (((1,), (1,)), ((), ())), preferred_element_type=F32
    )


def row_contract(left_op, right_op):
    return lax.dot_general(
        left_op, right_op, (((0,), (0,)), ((), ())), preferred_element_type=F32
    )


def block(start, size):
    return pl.ds(start if isinstance(start, int) else pl.multiple_of(start, 16), size)


def kernel(
    tok_ref, win_ref, wout_ref, gain_ref, cot_ref,
    mixed_ref, gin_ref, gwin_ref, gwout_ref,
    winc, woutc, xf, cf, pf, rf, pb, rb, slopes, hid, ghid,
    branch, zf, gnorm, zb, stat_out, stat_in, totals, scaled,
    dw, anti, near, qsum, far, tok_buf, win_buf, wout_buf, ssem, rsem, lsem,
):
    dp, z, h = lax.axis_index("dp"), lax.axis_index("tok"), lax.axis_index("hid")
    y, xh = dp // 2, dp % 2
    xl, c = h // 2, h % 2
    zp, zm = (dp, (z + 1) % N_TOK, h), (dp, (z + N_TOK - 1) % N_TOK, h)
    sib = (dp, z, xl * 2 + 1 - c)
    xn = (dp, z, (1 - xl) * 2 + c)
    diag = (dp, z, (1 - xl) * 2 + 1 - c)
    yp, ym = (((y + 1) % N_Y) * 2 + xh, z, h), (((y + N_Y - 1) % N_Y) * 2 + xh, z, h)
    xo = (y * 2 + 1 - xh, z, h)
    peers = (zp, zm, sib, xn, diag, yp, ym, xo)

    own_half, sib_half = c * WIDTH, (1 - c) * WIDTH
    lane_own = pl.ds(pl.multiple_of(own_half, WIDTH), WIDTH)
    lane_sib = pl.ds(pl.multiple_of(sib_half, WIDTH), WIDTH)

    barrier = pltpu.get_barrier_semaphore()
    for peer in peers:
        pl.semaphore_signal(barrier, inc=1, device_id=peer, device_id_type=MESH)

    local = [
        pltpu.make_async_copy(tok_ref, tok_buf, lsem.at[0]),
        pltpu.make_async_copy(cot_ref, cf.at[c, pl.ds(0, ROWS)], lsem.at[1]),
        pltpu.make_async_copy(wout_ref.at[lane_own, :], woutc.at[c], lsem.at[2]),
        pltpu.make_async_copy(win_ref.at[:, lane_own], winc.at[c], lsem.at[3]),
        pltpu.make_async_copy(wout_ref, wout_buf, lsem.at[4]),
        pltpu.make_async_copy(win_ref, win_buf, lsem.at[5]),
    ]
    for copy in local:
        copy.start()

    sent = []

    def send(src, dst, peer):
        i = len(sent)
        copy = pltpu.make_async_remote_copy(
            src_ref=src, dst_ref=dst, send_sem=ssem.at[i], recv_sem=rsem.at[i],
            device_id=peer, device_id_type=MESH,
        )
        copy.start()
        sent.append(copy)
        return copy

    def slot(r, lo=0, size=ROWS):
        return block(r * ROWS + lo, size)

    def ring_first(src, buf):
        return [
            (send(src, buf.at[c, slot(1)], zp),),
            (send(src, buf.at[c, slot(2)], zm),),
            send(src, buf.at[c, slot(0)], sib),
        ]

    ring = {"c": {}, "x": {}}
    sib_copies = {"c": {}, "x": {}}
    bufs = {"c": cf, "x": xf}

    def start_ring(name, src):
        up, down, across = ring_first(src, bufs[name])
        ring[name][1] = up + down
        sib_copies[name][0] = across

    def ring_wait(name, k):
        buf = bufs[name]
        for copy in ring[name][k]:
            copy.wait_recv()
        for r in (2 * k - 1, 2 * k) if k < 4 else (7,):
            sib_copies[name][r] = send(buf.at[c, slot(r)], buf.at[c, slot(r)], sib)

    def ring_forward(name, k):
        buf = bufs[name]
        a, b = 2 * k - 1, 2 * k
        if k < 3:
            ring[name][k + 1] = (
                send(buf.at[c, slot(a)], buf.at[c, slot(a + 2)], zp),
                send(buf.at[c, slot(b)], buf.at[c, slot(b + 2)], zm),
            )
        else:
            lo, hi = (0, SHARE), (SHARE, SHARE)
            ring[name][4] = (
                send(buf.at[c, slot(a, *lo)], buf.at[c, slot(7, *lo)], zp),
                send(buf.at[c, slot(b, *hi)], buf.at[c, slot(7, *hi)], zm),
            )

    lanes = lax.broadcasted_iota(jnp.int32, (ROWS, ROWS), 1)

    def share_stats(i, first, second):
        stat_out[i] = jnp.where(lanes == 0, first, second).T[0:8]
        return [
            send(stat_out.at[i], stat_in.at[i, j], peer)
            for j, peer in enumerate((xn, diag, sib))
        ]

    def total_stats(i, copies):
        for copy in copies:
            copy.wait_recv()
        total = (stat_out[i] + stat_in[i, 2]) + (stat_in[i, 0] + stat_in[i, 1])
        columns = jnp.concatenate([total] * (ROWS // 8), axis=0).T
        return columns[:, 0:1], columns[:, 1:2]

    local[0].wait()
    tok_float = tok_buf[...].astype(F32)
    tok_sum = jnp.sum(tok_float, axis=1, keepdims=True)
    tok_squares = jnp.sum(tok_float * tok_float, axis=1, keepdims=True)
    pl.semaphore_wait(barrier, len(peers))
    stats = share_stats(0, tok_sum, tok_squares)
    local[1].wait()
    start_ring("c", cf.at[c, slot(0)])
    weight_copies = [
        send(wout_ref.at[lane_sib, :], woutc.at[c], sib),
        send(win_ref.at[:, lane_sib], winc.at[c], sib),
    ]

    def partial_product(src, weights, dst, r, transposed):
        rows = slot(r)
        if transposed:
            total = right_contract(src[0, rows], weights[0])
            total += right_contract(src[1, rows], weights[1])
        else:
            total = dot(src[0, rows], weights[0]) + dot(src[1, rows], weights[1])
        dst[rows, :] = total.astype(BF16)

    partial_copies = {"f": {}, "b": {}}

    def send_partial(name, part, landing, r):
        partial_copies[name][r] = send(
            part.at[block(r * ROWS + (1 - xl) * SHARE, SHARE)],
            landing.at[block(r * SHARE, SHARE)],
            xn,
        )

    def f1(r):
        if r == 0:
            local[3].wait()
            weight_copies[1].wait_recv()
        sib_copies["x"][r].wait_recv()
        partial_product(xf, winc, pf, r, False)
        send_partial("f", pf, rf, r)

    def b1(r):
        if r == 0:
            local[2].wait()
            weight_copies[0].wait_recv()
        sib_copies["c"][r].wait_recv()
        partial_product(cf, woutc, pb, r, True)
        send_partial("b", pb, rb, r)

    share_copies = {"f": {}, "b": {}}
    whole_copies = {"f": {}, "b": {}}

    def send_share(name, buf, r):
        mine = buf.at[c, block(r * ROWS + xl * SHARE, SHARE)]
        share_copies[name][r] = send(mine, mine, xn)

    def f2(r):
        partial_copies["f"][r].wait_recv()

        def tile(n, carry):
            k = n * 16
            pre_act = pf[block(r * ROWS + xl * SHARE + k, 16), :].astype(F32)
            pre_act += rf[block(r * SHARE + k, 16), :].astype(F32)
            act, slope = gelu_pair(pre_act)
            slopes[block(r * SHARE + k, 16), :] = slope
            hid[c, block(r * ROWS + xl * SHARE + k, 16), :] = act.astype(BF16)
            return carry

        lax.fori_loop(0, SHARE // 16, tile, 0)
        send_share("f", hid, r)

    def b2(r):
        partial_copies["b"][r].wait_recv()

        def tile(n, carry):
            k = n * 16
            grad = pb[block(r * ROWS + xl * SHARE + k, 16), :].astype(F32)
            grad += rb[block(r * SHARE + k, 16), :].astype(F32)
            grad *= slopes[block(r * SHARE + k, 16), :]
            ghid[c, block(r * ROWS + xl * SHARE + k, 16), :] = grad.astype(BF16)
            return carry

        lax.fori_loop(0, SHARE // 16, tile, 0)
        send_share("b", ghid, r)

    def third(name, buf, r):
        share_copies[name][r].wait_recv()
        whole = buf.at[c, slot(r)]
        whole_copies[name][r] = send(whole, whole, sib)

    def f3(r):
        third("f", hid, r)

    def b3(r):
        third("b", ghid, r)

    waited = {"f": False, "b": False}

    def whole_wait(name):
        waited[name] = True
        for r in range(N_TOK):
            whole_copies[name][r].wait_recv()

    def product_rows(src, dst, i, transposed):
        if not waited["b" if transposed else "f"]:
            whole_wait("b" if transposed else "f")
        rows = block(i * 256, 256)
        if transposed:
            if i == 3:
                local[5].wait()
            total = right_contract(src[0, rows], win_buf[:, 0:WIDTH])
            total += right_contract(src[1, rows], win_buf[:, WIDTH : 2 * WIDTH])
        else:
            if i == 3:
                local[4].wait()
            total = dot(src[0, rows], wout_buf[0:WIDTH, :])
            total += dot(src[1, rows], wout_buf[WIDTH : 2 * WIDTH, :])
        dst[rows, :] = total.astype(BF16)

    def add_rows(dst, at, src, rows, count):
        def tile(n, carry):
            here = block(at + n * 16, 16)
            there = block(rows + n * 16, 16)
            dst[here, :] = (dst[here, :].astype(F32) + src[there, :].astype(F32)).astype(BF16)
            return carry

        lax.fori_loop(0, count // 16, tile, 0)

    back = {"f": {}, "b": {}}

    def ring_back(name, part, landing, k):
        if k == 4:
            back[name][4] = (
                send(part.at[slot(7, 0, SHARE)], landing.at[slot(5, 0, SHARE)], zm),
                send(part.at[slot(7, SHARE, SHARE)], landing.at[slot(6, SHARE, SHARE)], zp),
            )
            return
        a, b = 2 * k - 1, 2 * k
        for copy in back[name][k + 1]:
            copy.wait_recv()
        if k == 3:
            add_rows(part, a * ROWS, landing, a * ROWS, SHARE)
            add_rows(part, b * ROWS + SHARE, landing, b * ROWS + SHARE, SHARE)
        else:
            add_rows(part, a * ROWS, landing, a * ROWS, ROWS)
            add_rows(part, b * ROWS, landing, b * ROWS, ROWS)
        to_a, to_b = (0, 7) if k == 1 else (a - 2, b - 2)
        back[name][k] = (
            send(part.at[slot(a)], landing.at[slot(to_a)], zm),
            send(part.at[slot(b)], landing.at[slot(to_b)], zp),
        )

    def ring_total(name, part, landing):
        for copy in back[name][1]:
            copy.wait_recv()
        total = part[slot(0), :].astype(F32) + landing[slot(0), :].astype(F32)
        return total + landing[slot(7), :].astype(F32)

    qa, qb, qo = (y + 1) % N_Y, (y + N_Y - 1) % N_Y, (y + 2) % N_Y

    def weight_product(p):
        if p < 2:
            total = row_contract(hid[p], cf[c])
        else:
            total = row_contract(xf[c], ghid[p - 2])
        dw[p] = (total * GRAD_SCALE).astype(BF16)

    first_hop, second_hop, far_copies, spread, spread_on, across = {}, {}, {}, {}, {}, {}
    low, high = block(0, EIGHTH), block(EIGHTH, EIGHTH)

    def r1(p):
        part = dw.at[p]
        first_hop[p] = (
            send(part.at[block(qo * QUARTER, EIGHTH)], anti.at[p, low], yp),
            send(part.at[block(qo * QUARTER + EIGHTH, EIGHTH)], anti.at[p, high], ym),
        )
        second_hop[p] = (
            send(part.at[block(qa * QUARTER + EIGHTH, EIGHTH)], near.at[p, 0, high], yp),
            send(part.at[block(qb * QUARTER, EIGHTH)], near.at[p, 1, low], ym),
        )

    def r2(p):
        part = dw.at[p]
        for copy in first_hop[p]:
            copy.wait_recv()
        add_rows(part, qa * QUARTER, anti.at[p], 0, EIGHTH)
        add_rows(part, qb * QUARTER + EIGHTH, anti.at[p], EIGHTH, EIGHTH)
        second_hop[p] += (
            send(part.at[block(qa * QUARTER, EIGHTH)], near.at[p, 0, low], yp),
            send(part.at[block(qb * QUARTER + EIGHTH, EIGHTH)], near.at[p, 1, high], ym),
        )

    def r3(p):
        for copy in second_hop[p]:
            copy.wait_recv()

        def tile(n, carry):
            rows = block(n * 16, 16)
            total = dw[p, block(y * QUARTER + n * 16, 16), :].astype(F32)
            total += near[p, 0, rows, :].astype(F32) + near[p, 1, rows, :].astype(F32)
            qsum[p, rows, :] = total.astype(BF16)
            return carry

        lax.fori_loop(0, QUARTER // 16, tile, 0)
        if p in X_LAST:
            theirs = block((1 - xh) * EIGHTH, EIGHTH)
            far_copies[p] = send(qsum.at[p, theirs], far.at[p, low], xo)
        else:
            far_copies[p] = send(qsum.at[p], far.at[p], xo)

    def out_rows(p, start, size):
        if p < 2:
            return gwout_ref, (block(p * WIDTH + start, size), slice(None))
        return gwin_ref, (block(start, size), pl.ds((p - 2) * WIDTH, WIDTH))

    def out_at(p, start, size):
        ref, where = out_rows(p, start, size)
        return ref.at[where]

    def r4(p):
        far_copies[p].wait_recv()
        mine, count = (xh * EIGHTH, EIGHTH) if p in X_LAST else (0, QUARTER)

        def tile(n, carry):
            total = qsum[p, block(mine + n * 16, 16), :].astype(F32)
            total += far[p, block(n * 16, 16), :].astype(F32)
            ref, where = out_rows(p, y * QUARTER + mine + n * 16, 16)
            ref[where] = total.astype(BF16)
            return carry

        lax.fori_loop(0, count // 16, tile, 0)
        own = out_at(p, y * QUARTER + mine, count)
        spread[p] = (send(own, own, yp), send(own, own, ym))
        if p in X_LAST:
            across[p] = (send(own, own, xo),)

    def r5(p):
        for copy in spread[p]:
            copy.wait_recv()
        mine, half = (xh * EIGHTH, EIGHTH // 2) if p in X_LAST else (0, EIGHTH)
        behind = out_at(p, qb * QUARTER + mine, half)
        ahead = out_at(p, qa * QUARTER + mine + half, half)
        spread_on[p] = (send(behind, behind, yp), send(ahead, ahead, ym))
        if p in X_LAST:
            for q in (qb, qa):
                whole = out_at(p, q * QUARTER + mine, EIGHTH)
                across[p] += (send(whole, whole, xo),)

    def r6(p):
        for copy in spread_on[p]:
            copy.wait_recv()
        if p in X_LAST:
            whole = out_at(p, qo * QUARTER + xh * EIGHTH, EIGHTH)
            across[p] += (send(whole, whole, xo),)

    def r7(p):
        for copy in across[p]:
            copy.wait_recv()

    state = {}

    def normalize():
        row_sum, square_sum = total_stats(0, stats)
        row_mean = row_sum / D
        row_rstd = lax.rsqrt(square_sum / D - row_mean * row_mean + norm_eps)
        totals[...] = jnp.where(lanes == 0, row_mean, row_rstd)
        centred = (tok_float - row_mean) * row_rstd
        xf[c, slot(0)] = (centred * gain_ref[...]).astype(BF16)
        start_ring("x", xf.at[c, slot(0)])

    def blk(name, i):
        if name == "f":
            product_rows(hid, branch, i, False)
        else:
            product_rows(ghid, gnorm, i, True)

    def back_step(name, k):
        if name == "f":
            ring_back(name, branch, zf, k)
        else:
            ring_back(name, gnorm, zb, k)

    def finish_out():
        mixed_ref[...] = (
            tok_buf[...].astype(F32) + ring_total("f", branch, zf)
        ).astype(BF16)

    def centred_rows():
        row_mean, row_rstd = totals[:, 0:1], totals[:, 1:2]
        return (tok_buf[...].astype(F32) - row_mean) * row_rstd, row_rstd

    def share_grad():
        grad_scaled = ring_total("b", gnorm, zb) * gain_ref[...]
        scaled[...] = grad_scaled
        centred, _ = centred_rows()
        state["grad"] = share_stats(
            1,
            jnp.sum(grad_scaled, axis=1, keepdims=True),
            jnp.sum(grad_scaled * centred, axis=1, keepdims=True),
        )

    def finish_grad():
        first_sum, second_sum = total_stats(1, state["grad"])
        centred, row_rstd = centred_rows()
        gin_ref[...] = (
            cf[c, slot(0)].astype(F32)
            + row_rstd * (scaled[...] - first_sum / D - centred * (second_sum / D))
        ).astype(BF16)

    def product(p):
        if p in (0, 1) and not waited["f"]:
            whole_wait("f")
        if p in (2, 3) and not waited["b"]:
            whole_wait("b")
        weight_product(p)
        r1(p)

    schedule = (
        (b1, 0), (normalize,), (ring_wait, "c", 1), (f1, 0), (b1, 2), (f2, 0), (ring_wait, "x", 1), (f1, 2),
        (ring_forward, "x", 1), (f1, 1), (f2, 2), (ring_wait, "x", 2), (ring_forward, "x", 2), (f2, 1),
        (f1, 3), (ring_forward, "c", 1), (f1, 4), (ring_wait, "x", 3), (f2, 3), (f3, 1), (f1, 6), (f1, 5),
        (f2, 4), (ring_wait, "c", 2), (ring_forward, "x", 3), (f3, 2), (ring_wait, "x", 4), (f3, 3),
        (ring_forward, "c", 2), (f1, 7), (f2, 5), (f2, 7), (ring_wait, "c", 3), (f2, 6), (f3, 0), (b1, 3),
        (f3, 7), (ring_forward, "c", 3), (f3, 4), (b2, 2), (f3, 5), (b2, 0), (f3, 6), (b1, 1), (blk, "f", 3),
        (ring_wait, "c", 4), (b1, 6), (b1, 5), (b1, 4), (b2, 3), (product, 1), (b2, 1), (b3, 2), (r2, 1),
        (b2, 6), (b1, 7), (blk, "f", 2), (product, 0), (r3, 1), (b2, 7), (b3, 3), (back_step, "f", 4),
        (b3, 1), (b3, 6), (b2, 5), (b2, 4), (r2, 0), (b3, 0), (r4, 1), (b3, 5), (blk, "f", 1), (b3, 7),
        (r3, 0), (r5, 1), (b3, 4), (product, 2), (r2, 2), (back_step, "f", 3), (blk, "f", 0), (blk, "b", 3),
        (product, 3), (back_step, "f", 2), (blk, "b", 1), (r3, 2), (blk, "b", 2), (blk, "b", 0), (r2, 3),
        (back_step, "b", 4), (r4, 2), (back_step, "b", 3), (r4, 0), (r3, 3), (back_step, "b", 2), (r5, 2),
        (r4, 3), (r6, 1), (back_step, "b", 1), (r5, 0), (back_step, "f", 1), (r6, 2), (share_grad,), (r5, 3),
        (finish_grad,), (finish_out,), (r6, 0), (r7, 2), (r7, 1), (r6, 3),
    )
    for step, *where in schedule:
        step(*where)
    for copy in sent:
        copy.wait_send()


def shards(tokens, w_in, w_out, gain, cotangent):
    vmem = pl.BlockSpec(memory_space=pltpu.VMEM)
    anywhere = pl.BlockSpec(memory_space=pl.ANY)
    return pl.pallas_call(
        kernel,
        out_shape=(
            pltpu.VMEM((ROWS, WIDTH), BF16),
            pltpu.VMEM((ROWS, WIDTH), BF16),
            pltpu.VMEM((WIDTH, 2 * WIDTH), BF16),
            pltpu.VMEM((2 * WIDTH, WIDTH), BF16),
        ),
        in_specs=[anywhere, anywhere, anywhere, vmem, anywhere],
        out_specs=(vmem,) * 4,
        scratch_shapes=[
            pltpu.VMEM((2, WIDTH, WIDTH), BF16),
            pltpu.VMEM((2, WIDTH, WIDTH), BF16),
            pltpu.VMEM((2, TOK, WIDTH), BF16),
            pltpu.VMEM((2, TOK, WIDTH), BF16),
            pltpu.VMEM((TOK, WIDTH), BF16),
            pltpu.VMEM((TOK // 2, WIDTH), BF16),
            pltpu.VMEM((TOK, WIDTH), BF16),
            pltpu.VMEM((TOK // 2, WIDTH), BF16),
            pltpu.VMEM((TOK // 2, WIDTH), F32),
            pltpu.VMEM((2, TOK, WIDTH), BF16),
            pltpu.VMEM((2, TOK, WIDTH), BF16),
            pltpu.VMEM((TOK, WIDTH), BF16),
            pltpu.VMEM((TOK, WIDTH), BF16),
            pltpu.VMEM((TOK, WIDTH), BF16),
            pltpu.VMEM((TOK, WIDTH), BF16),
            pltpu.VMEM((2, 8, ROWS), F32),
            pltpu.VMEM((2, 3, 8, ROWS), F32),
            pltpu.VMEM((ROWS, ROWS), F32),
            pltpu.VMEM((ROWS, WIDTH), F32),
            pltpu.VMEM((PIECES, WIDTH, WIDTH), BF16),
            pltpu.VMEM((PIECES, QUARTER, WIDTH), BF16),
            pltpu.VMEM((PIECES, 2, QUARTER, WIDTH), BF16),
            pltpu.VMEM((PIECES, QUARTER, WIDTH), BF16),
            pltpu.VMEM((PIECES, QUARTER, WIDTH), BF16),
            pltpu.VMEM((ROWS, WIDTH), BF16),
            pltpu.VMEM((WIDTH, 2 * WIDTH), BF16),
            pltpu.VMEM((2 * WIDTH, WIDTH), BF16),
            pltpu.SemaphoreType.DMA((MAX_COPIES,)),
            pltpu.SemaphoreType.DMA((MAX_COPIES,)),
            pltpu.SemaphoreType.DMA((6,)),
        ],
        compiler_params=pltpu.CompilerParams(
            collective_id=0, has_side_effects=True, vmem_limit_bytes=54 << 20
        ),
        cost_estimate=pl.CostEstimate(
            flops=6 * 2 * TOK * WIDTH * 2 * WIDTH, bytes_accessed=12 << 20, transcendentals=0
        ),
        name="mlp_block",
    )(tokens, w_in, w_out, gain.reshape(1, WIDTH), cotangent)


def solution(mesh):
    in_specs = (
        P(("dp", "tok"), "hid"),
        P("hid", "tok"),
        P("tok", "hid"),
        P("hid"),
        P(("dp", "tok"), "hid"),
    )
    out_specs = (P(("dp", "tok"), "hid"), P(("dp", "tok"), "hid"), P("hid", "tok"), P("tok", "hid"))
    return jax.shard_map(shards, mesh=mesh, in_specs=in_specs, out_specs=out_specs, check_vma=False)
```

```python
import functools
import math

import jax
import jax.numpy as jnp
from jax import lax
from jax.experimental import pallas as pl
from jax.experimental.pallas import tpu as pltpu
from jax.sharding import PartitionSpec as P

D = 3072
ROWS = 128
WIDTH = 768
TOK = 1024
N_TOK = 8
N_Y = 4
QUARTER = WIDTH // N_Y
EIGHTH = QUARTER // 2
SHARE = ROWS // 2
PIECES = 4
X_LAST = (2, 3)
MAX_COPIES = 220
SUB = WIDTH // 2
GROUPS = ((0, 128), (128, 256), (384, 256), (640, 256), (896, 128))

norm_eps = 1e-06
GRAD_SCALE = 1.0 / math.sqrt(8192)
MESH = pl.DeviceIdType.MESH
BF16 = jnp.bfloat16
F32 = jnp.float32


def gelu_pair(pre_act):
    cdf_part = 0.5 * (1.0 + lax.erf(pre_act * (1.0 / math.sqrt(2.0))))
    dens_part = jnp.exp(-0.5 * pre_act * pre_act) * (1.0 / math.sqrt(2.0 * math.pi))
    return (pre_act * cdf_part, cdf_part + pre_act * dens_part)


def dot(left_op, right_op):
    return jnp.dot(left_op, right_op, preferred_element_type=F32)


def right_contract(left_op, right_op):
    return lax.dot_general(
        left_op, right_op, (((1,), (1,)), ((), ())), preferred_element_type=F32
    )


def row_contract(left_op, right_op):
    return lax.dot_general(
        left_op, right_op, (((0,), (0,)), ((), ())), preferred_element_type=F32
    )


def block(start, size):
    return pl.ds(start if isinstance(start, int) else pl.multiple_of(start, 16), size)


def kernel(
    tok_ref, win_ref, wout_ref, gain_ref, cot_ref,
    mixed_ref, gin_ref, pieces_ref,
    winc, woutc, xf, cf, pf, rf, pb, rb, slopes, hid, ghid,
    branch, zf, gnorm, zb, stat_out, stat_in, totals, scaled,
    dw, anti, near, qsum, far, tok_buf, win_buf, wout_buf, ssem, rsem, lsem,
):
    dp, z, h = lax.axis_index("dp"), lax.axis_index("tok"), lax.axis_index("hid")
    y, xh = dp // 2, dp % 2
    xl, c = h // 2, h % 2
    zp, zm = (dp, (z + 1) % N_TOK, h), (dp, (z + N_TOK - 1) % N_TOK, h)
    sib = (dp, z, xl * 2 + 1 - c)
    xn = (dp, z, (1 - xl) * 2 + c)
    diag = (dp, z, (1 - xl) * 2 + 1 - c)
    yp, ym = (((y + 1) % N_Y) * 2 + xh, z, h), (((y + N_Y - 1) % N_Y) * 2 + xh, z, h)
    xo = (y * 2 + 1 - xh, z, h)
    peers = (zp, zm, sib, xn, diag, yp, ym, xo)

    own_half, sib_half = c * WIDTH, (1 - c) * WIDTH
    lane_own = pl.ds(pl.multiple_of(own_half, WIDTH), WIDTH)
    lane_sib = pl.ds(pl.multiple_of(sib_half, WIDTH), WIDTH)

    barrier = pltpu.get_barrier_semaphore()
    for peer in peers:
        pl.semaphore_signal(barrier, inc=1, device_id=peer, device_id_type=MESH)

    local = [
        pltpu.make_async_copy(tok_ref, tok_buf, lsem.at[0]),
        pltpu.make_async_copy(cot_ref, cf.at[c, pl.ds(0, ROWS)], lsem.at[1]),
        pltpu.make_async_copy(wout_ref.at[lane_own, :], woutc.at[c], lsem.at[2]),
        pltpu.make_async_copy(win_ref.at[:, lane_own], winc.at[c], lsem.at[3]),
        pltpu.make_async_copy(wout_ref, wout_buf, lsem.at[4]),
        pltpu.make_async_copy(win_ref, win_buf, lsem.at[5]),
    ]
    for copy in local:
        copy.start()

    sent = []

    def send(src, dst, peer):
        i = len(sent)
        copy = pltpu.make_async_remote_copy(
            src_ref=src, dst_ref=dst, send_sem=ssem.at[i], recv_sem=rsem.at[i],
            device_id=peer, device_id_type=MESH,
        )
        copy.start()
        sent.append(copy)
        return copy

    def slot(r, lo=0, size=ROWS):
        return block(r * ROWS + lo, size)

    def ring_first(src, buf):
        return [
            (send(src, buf.at[c, slot(1)], zp),),
            (send(src, buf.at[c, slot(2)], zm),),
            send(src, buf.at[c, slot(0)], sib),
        ]

    ring = {"c": {}, "x": {}}
    sib_copies = {"c": {}, "x": {}}
    bufs = {"c": cf, "x": xf}

    def start_ring(name, src):
        up, down, across = ring_first(src, bufs[name])
        ring[name][1] = up + down
        sib_copies[name][0] = across

    def ring_wait(name, k):
        buf = bufs[name]
        for copy in ring[name][k]:
            copy.wait_recv()
        rows = block(*GROUPS[k])
        sib_copies[name][k] = send(buf.at[c, rows], buf.at[c, rows], sib)

    def ring_forward(name, k):
        buf = bufs[name]
        a, b = 2 * k - 1, 2 * k
        if k < 3:
            ring[name][k + 1] = (
                send(buf.at[c, slot(a)], buf.at[c, slot(a + 2)], zp),
                send(buf.at[c, slot(b)], buf.at[c, slot(b + 2)], zm),
            )
        else:
            lo, hi = (0, SHARE), (SHARE, SHARE)
            ring[name][4] = (
                send(buf.at[c, slot(a, *lo)], buf.at[c, slot(7, *lo)], zp),
                send(buf.at[c, slot(b, *hi)], buf.at[c, slot(7, *hi)], zm),
            )

    lanes = lax.broadcasted_iota(jnp.int32, (ROWS, ROWS), 1)

    def share_stats(i, first, second):
        stat_out[i] = jnp.where(lanes == 0, first, second).T[0:8]
        return [
            send(stat_out.at[i], stat_in.at[i, j], peer)
            for j, peer in enumerate((xn, diag, sib))
        ]

    def total_stats(i, copies):
        for copy in copies:
            copy.wait_recv()
        total = (stat_out[i] + stat_in[i, 2]) + (stat_in[i, 0] + stat_in[i, 1])
        columns = jnp.concatenate([total] * (ROWS // 8), axis=0).T
        return columns[:, 0:1], columns[:, 1:2]

    local[0].wait()
    tok_float = tok_buf[...].astype(F32)
    tok_sum = jnp.sum(tok_float, axis=1, keepdims=True)
    tok_squares = jnp.sum(tok_float * tok_float, axis=1, keepdims=True)
    pl.semaphore_wait(barrier, len(peers))
    stats = share_stats(0, tok_sum, tok_squares)
    local[1].wait()
    start_ring("c", cf.at[c, slot(0)])
    weight_copies = [
        send(wout_ref.at[lane_sib, :], woutc.at[c], sib),
        send(win_ref.at[:, lane_sib], winc.at[c], sib),
    ]

    def sub(part):
        return pl.ds(part * SUB, SUB)

    arrived = set()

    def arrive(key, *waits):
        if key not in arrived:
            arrived.add(key)
            for wait in waits:
                wait()

    partial_copies = {"f": {}, "b": {}}
    share_copies = {"f": {}, "b": {}}
    whole_copies = {"f": {}, "b": {}}

    def send_partial(name, part, landing, g, u):
        start, count = GROUPS[g]
        half = count // 2
        partial_copies[name][g, u] = send(
            part.at[block(start + (1 - xl) * half, half), sub(u)],
            landing.at[block(start // 2, half), sub(u)],
            xn,
        )

    def send_share(name, buf, g, u):
        start, count = GROUPS[g]
        half = count // 2
        mine = buf.at[c, block(start + xl * half, half), sub(u)]
        share_copies[name][g, u] = send(mine, mine, xn)

    def f1(g, u):
        arrive("win", local[3].wait, weight_copies[1].wait_recv)
        arrive(("x", g), sib_copies["x"][g].wait_recv)
        rows, cols = block(*GROUPS[g]), sub(u)
        total = dot(xf[0, rows], winc[0, :, cols]) + dot(xf[1, rows], winc[1, :, cols])
        pf[rows, cols] = total.astype(BF16)
        send_partial("f", pf, rf, g, u)

    def b1(g, u):
        arrive("wout", local[2].wait, weight_copies[0].wait_recv)
        arrive(("c", g), sib_copies["c"][g].wait_recv)
        rows, cols = block(*GROUPS[g]), sub(u)
        total = right_contract(cf[0, rows], woutc[0, cols, :])
        total += right_contract(cf[1, rows], woutc[1, cols, :])
        pb[rows, cols] = total.astype(BF16)
        send_partial("b", pb, rb, g, u)

    def f2(g, u):
        partial_copies["f"][g, u].wait_recv()
        start, count = GROUPS[g]
        mine, landed = start + xl * (count // 2), start // 2

        def tile(n, carry):
            k = n * 32
            pre_act = pf[block(mine + k, 32), sub(u)].astype(F32)
            pre_act += rf[block(landed + k, 32), sub(u)].astype(F32)
            act, slope = gelu_pair(pre_act)
            slopes[block(landed + k, 32), sub(u)] = slope
            hid[c, block(mine + k, 32), sub(u)] = act.astype(BF16)
            return carry

        lax.fori_loop(0, count // 64, tile, 0)
        send_share("f", hid, g, u)

    def b2(g, u):
        partial_copies["b"][g, u].wait_recv()
        start, count = GROUPS[g]
        mine, landed = start + xl * (count // 2), start // 2

        def tile(n, carry):
            k = n * 32
            grad = pb[block(mine + k, 32), sub(u)].astype(F32)
            grad += rb[block(landed + k, 32), sub(u)].astype(F32)
            grad *= slopes[block(landed + k, 32), sub(u)]
            ghid[c, block(mine + k, 32), sub(u)] = grad.astype(BF16)
            return carry

        lax.fori_loop(0, count // 64, tile, 0)
        send_share("b", ghid, g, u)

    def third(name, buf, g, u):
        share_copies[name][g, u].wait_recv()
        whole = buf.at[c, block(*GROUPS[g]), sub(u)]
        whole_copies[name][g, u] = send(whole, whole, sib)

    def f3(g, u):
        third("f", hid, g, u)

    def b3(g, u):
        third("b", ghid, g, u)

    def whole_wait(name, u):
        waits = [whole_copies[name][g, u].wait_recv for g in range(len(GROUPS))]
        arrive((name, "whole", u), *waits)

    def product_rows(src, dst, i, transposed):
        for u in range(2):
            whole_wait("b" if transposed else "f", u)
        rows = block(i * 256, 256)
        if transposed:
            arrive("win_buf", local[5].wait)
            total = right_contract(src[0, rows], win_buf[:, 0:WIDTH])
            total += right_contract(src[1, rows], win_buf[:, WIDTH : 2 * WIDTH])
        else:
            arrive("wout_buf", local[4].wait)
            total = dot(src[0, rows], wout_buf[0:WIDTH, :])
            total += dot(src[1, rows], wout_buf[WIDTH : 2 * WIDTH, :])
        dst[rows, :] = total.astype(BF16)

    def add_rows(dst, at, src, rows, count):
        def tile(n, carry):
            here = block(at + n * 16, 16)
            there = block(rows + n * 16, 16)
            dst[here, :] = (dst[here, :].astype(F32) + src[there, :].astype(F32)).astype(BF16)
            return carry

        lax.fori_loop(0, count // 16, tile, 0)

    back = {"f": {}, "b": {}}

    def ring_back(name, part, landing, k):
        if k == 4:
            back[name][4] = (
                send(part.at[slot(7, 0, SHARE)], landing.at[slot(5, 0, SHARE)], zm),
                send(part.at[slot(7, SHARE, SHARE)], landing.at[slot(6, SHARE, SHARE)], zp),
            )
            return
        a, b = 2 * k - 1, 2 * k
        for copy in back[name][k + 1]:
            copy.wait_recv()
        if k == 3:
            add_rows(part, a * ROWS, landing, a * ROWS, SHARE)
            add_rows(part, b * ROWS + SHARE, landing, b * ROWS + SHARE, SHARE)
        else:
            add_rows(part, a * ROWS, landing, a * ROWS, ROWS)
            add_rows(part, b * ROWS, landing, b * ROWS, ROWS)
        to_a, to_b = (0, 7) if k == 1 else (a - 2, b - 2)
        back[name][k] = (
            send(part.at[slot(a)], landing.at[slot(to_a)], zm),
            send(part.at[slot(b)], landing.at[slot(to_b)], zp),
        )

    def ring_total(name, part, landing):
        for copy in back[name][1]:
            copy.wait_recv()
        total = part[slot(0), :].astype(F32) + landing[slot(0), :].astype(F32)
        return total + landing[slot(7), :].astype(F32)

    qa, qb, qo = (y + 1) % N_Y, (y + N_Y - 1) % N_Y, (y + 2) % N_Y

    def weight_product(p):
        cols = sub(p % 2)
        for core in range(2):
            half = sub(core)
            if p < 2:
                total = row_contract(hid[core, :, cols], cf[c])
                dw[p, half, :] = (total * GRAD_SCALE).astype(BF16)
            else:
                total = row_contract(xf[c], ghid[core, :, cols])
                dw[p, :, half] = (total * GRAD_SCALE).astype(BF16)

    first_hop, second_hop, far_copies, spread, spread_on, across = {}, {}, {}, {}, {}, {}
    low, high = block(0, EIGHTH), block(EIGHTH, EIGHTH)

    def r1(p):
        part = dw.at[p]
        first_hop[p] = (
            send(part.at[block(qo * QUARTER, EIGHTH)], anti.at[p, low], yp),
            send(part.at[block(qo * QUARTER + EIGHTH, EIGHTH)], anti.at[p, high], ym),
        )
        second_hop[p] = (
            send(part.at[block(qa * QUARTER + EIGHTH, EIGHTH)], near.at[p, 0, high], yp),
            send(part.at[block(qb * QUARTER, EIGHTH)], near.at[p, 1, low], ym),
        )

    def r2(p):
        part = dw.at[p]
        for copy in first_hop[p]:
            copy.wait_recv()
        add_rows(part, qa * QUARTER, anti.at[p], 0, EIGHTH)
        add_rows(part, qb * QUARTER + EIGHTH, anti.at[p], EIGHTH, EIGHTH)
        second_hop[p] += (
            send(part.at[block(qa * QUARTER, EIGHTH)], near.at[p, 0, low], yp),
            send(part.at[block(qb * QUARTER + EIGHTH, EIGHTH)], near.at[p, 1, high], ym),
        )

    def r3(p):
        for copy in second_hop[p]:
            copy.wait_recv()

        def tile(n, carry):
            rows = block(n * 16, 16)
            total = dw[p, block(y * QUARTER + n * 16, 16), :].astype(F32)
            total += near[p, 0, rows, :].astype(F32) + near[p, 1, rows, :].astype(F32)
            qsum[p, rows, :] = total.astype(BF16)
            return carry

        lax.fori_loop(0, QUARTER // 16, tile, 0)
        if p in X_LAST:
            theirs = block((1 - xh) * EIGHTH, EIGHTH)
            far_copies[p] = send(qsum.at[p, theirs], far.at[p, low], xo)
        else:
            far_copies[p] = send(qsum.at[p], far.at[p], xo)

    def out_at(p, start, size):
        return pieces_ref.at[p, block(start, size)]

    def r4(p):
        far_copies[p].wait_recv()
        mine, count = (xh * EIGHTH, EIGHTH) if p in X_LAST else (0, QUARTER)

        def tile(n, carry):
            total = qsum[p, block(mine + n * 16, 16), :].astype(F32)
            total += far[p, block(n * 16, 16), :].astype(F32)
            pieces_ref[p, block(y * QUARTER + mine + n * 16, 16), :] = total.astype(BF16)
            return carry

        lax.fori_loop(0, count // 16, tile, 0)
        own = out_at(p, y * QUARTER + mine, count)
        spread[p] = (send(own, own, yp), send(own, own, ym))
        if p in X_LAST:
            across[p] = (send(own, own, xo),)

    def r5(p):
        for copy in spread[p]:
            copy.wait_recv()
        mine, half = (xh * EIGHTH, EIGHTH // 2) if p in X_LAST else (0, EIGHTH)
        behind = out_at(p, qb * QUARTER + mine, half)
        ahead = out_at(p, qa * QUARTER + mine + half, half)
        spread_on[p] = (send(behind, behind, yp), send(ahead, ahead, ym))
        if p in X_LAST:
            for q in (qb, qa):
                whole = out_at(p, q * QUARTER + mine, EIGHTH)
                across[p] += (send(whole, whole, xo),)

    def r6(p):
        for copy in spread_on[p]:
            copy.wait_recv()
        if p in X_LAST:
            whole = out_at(p, qo * QUARTER + xh * EIGHTH, EIGHTH)
            across[p] += (send(whole, whole, xo),)

    def r7(p):
        for copy in across[p]:
            copy.wait_recv()

    state = {}

    def normalize():
        row_sum, square_sum = total_stats(0, stats)
        row_mean = row_sum / D
        row_rstd = lax.rsqrt(square_sum / D - row_mean * row_mean + norm_eps)
        totals[...] = jnp.where(lanes == 0, row_mean, row_rstd)
        centred = (tok_float - row_mean) * row_rstd
        xf[c, slot(0)] = (centred * gain_ref[...][None, :]).astype(BF16)
        start_ring("x", xf.at[c, slot(0)])

    def blk(name, i):
        if name == "f":
            product_rows(hid, branch, i, False)
        else:
            product_rows(ghid, gnorm, i, True)

    def back_step(name, k):
        if name == "f":
            ring_back(name, branch, zf, k)
        else:
            ring_back(name, gnorm, zb, k)

    def finish_out():
        mixed_ref[...] = (
            tok_buf[...].astype(F32) + ring_total("f", branch, zf)
        ).astype(BF16)

    def centred_rows():
        row_mean, row_rstd = totals[:, 0:1], totals[:, 1:2]
        return (tok_buf[...].astype(F32) - row_mean) * row_rstd, row_rstd

    def share_grad():
        grad_scaled = ring_total("b", gnorm, zb) * gain_ref[...][None, :]
        scaled[...] = grad_scaled
        centred, _ = centred_rows()
        state["grad"] = share_stats(
            1,
            jnp.sum(grad_scaled, axis=1, keepdims=True),
            jnp.sum(grad_scaled * centred, axis=1, keepdims=True),
        )

    def finish_grad():
        first_sum, second_sum = total_stats(1, state["grad"])
        centred, row_rstd = centred_rows()
        gin_ref[...] = (
            cf[c, slot(0)].astype(F32)
            + row_rstd * (scaled[...] - first_sum / D - centred * (second_sum / D))
        ).astype(BF16)

    def product(p):
        whole_wait("f" if p < 2 else "b", p % 2)
        weight_product(p)
        r1(p)

    schedule = (
        (normalize,), (b1, 0, 0), (b1, 0, 1), (ring_wait, "c", 1), (f1, 0, 1), (f1, 0, 0), (b1, 1, 1),
        (ring_forward, "c", 1), (ring_wait, "x", 1), (f2, 0, 0), (f1, 1, 0), (f2, 0, 1),
        (ring_forward, "x", 1), (f1, 1, 1), (f2, 1, 0), (ring_wait, "x", 2), (ring_wait, "c", 2), (f2, 1, 1),
        (ring_forward, "x", 2), (f1, 2, 1), (f3, 1, 1), (b1, 1, 0), (f1, 2, 0), (ring_wait, "x", 3),
        (ring_forward, "x", 3), (f1, 3, 0), (b2, 0, 0), (ring_wait, "x", 4), (f3, 0, 0), (f2, 2, 1),
        (f2, 3, 0), (f3, 1, 0), (f1, 4, 0), (ring_forward, "c", 2), (f1, 3, 1), (f1, 4, 1),
        (ring_wait, "c", 3), (b3, 0, 0), (ring_forward, "c", 3), (f2, 2, 0), (f3, 0, 1), (f2, 4, 0),
        (f2, 4, 1), (ring_wait, "c", 4), (f2, 3, 1), (f3, 3, 0), (f3, 2, 0), (b1, 3, 1), (b2, 1, 0),
        (f3, 4, 0), (product, 0), (b1, 2, 0), (f3, 3, 1), (f3, 4, 1), (b1, 4, 0), (b1, 3, 0), (b3, 1, 0),
        (f3, 2, 1), (r2, 0), (product, 1), (b2, 0, 1), (b2, 4, 0), (b2, 3, 0), (b2, 2, 0), (b2, 1, 1),
        (b3, 3, 0), (b1, 2, 1), (b3, 0, 1), (blk, "f", 3), (b2, 3, 1), (b3, 4, 0), (r2, 1), (b3, 2, 0),
        (product, 2), (b1, 4, 1), (b2, 2, 1), (blk, "f", 0), (b2, 4, 1), (r3, 1), (b3, 3, 1), (b3, 1, 1),
        (back_step, "f", 4), (r2, 2), (b3, 2, 1), (b3, 4, 1), (product, 3), (r3, 2), (blk, "b", 3),
        (back_step, "b", 4), (r3, 0), (blk, "f", 1), (blk, "b", 1), (blk, "b", 2), (r2, 3), (blk, "f", 2),
        (back_step, "f", 3), (back_step, "b", 3), (blk, "b", 0), (r4, 2), (r3, 3), (r5, 2),
        (back_step, "f", 2), (r4, 1), (back_step, "f", 1), (r6, 2), (r4, 3), (r5, 1), (r5, 3), (finish_out,),
        (back_step, "b", 2), (r4, 0), (back_step, "b", 1), (r6, 3), (r7, 2), (r5, 0), (share_grad,), (r6, 1),
        (finish_grad,), (r6, 0), (r7, 3),
    )
    for step, *where in schedule:
        step(*where)
    for copy in sent:
        copy.wait_send()


def write_out(mixed_in, gin_in, pieces, mixed_ref, gin_ref, gwin_ref, gwout_ref, sems):
    pairs = [(mixed_in, mixed_ref), (gin_in, gin_ref)]
    for p in range(PIECES):
        for core in range(2):
            half = pl.ds(core * SUB, SUB)
            place = pl.ds(core * WIDTH + (p % 2) * SUB, SUB)
            if p < 2:
                pairs.append((pieces.at[p, half, :], gwout_ref.at[place, :]))
            else:
                pairs.append((pieces.at[p, :, half], gwin_ref.at[:, place]))
    copies = [
        pltpu.make_async_copy(src, dst, sems.at[i]) for i, (src, dst) in enumerate(pairs)
    ]
    for copy in copies:
        copy.start()
    for copy in copies:
        copy.wait()


def shards(tokens, w_in, w_out, gain, cotangent):
    vmem = pl.BlockSpec(memory_space=pltpu.VMEM)
    anywhere = pl.BlockSpec(memory_space=pl.ANY)
    mixed, grad_input, pieces = pl.pallas_call(
        kernel,
        out_shape=(
            pltpu.VMEM((ROWS, WIDTH), BF16),
            pltpu.VMEM((ROWS, WIDTH), BF16),
            pltpu.VMEM((PIECES, WIDTH, WIDTH), BF16),
        ),
        in_specs=[anywhere, anywhere, anywhere, vmem, anywhere],
        out_specs=(vmem,) * 3,
        scratch_shapes=[
            pltpu.VMEM((2, WIDTH, WIDTH), BF16),
            pltpu.VMEM((2, WIDTH, WIDTH), BF16),
            pltpu.VMEM((2, TOK, WIDTH), BF16),
            pltpu.VMEM((2, TOK, WIDTH), BF16),
            pltpu.VMEM((TOK, WIDTH), BF16),
            pltpu.VMEM((TOK // 2, WIDTH), BF16),
            pltpu.VMEM((TOK, WIDTH), BF16),
            pltpu.VMEM((TOK // 2, WIDTH), BF16),
            pltpu.VMEM((TOK // 2, WIDTH), F32),
            pltpu.VMEM((2, TOK, WIDTH), BF16),
            pltpu.VMEM((2, TOK, WIDTH), BF16),
            pltpu.VMEM((TOK, WIDTH), BF16),
            pltpu.VMEM((TOK, WIDTH), BF16),
            pltpu.VMEM((TOK, WIDTH), BF16),
            pltpu.VMEM((TOK, WIDTH), BF16),
            pltpu.VMEM((2, 8, ROWS), F32),
            pltpu.VMEM((2, 3, 8, ROWS), F32),
            pltpu.VMEM((ROWS, ROWS), F32),
            pltpu.VMEM((ROWS, WIDTH), F32),
            pltpu.VMEM((PIECES, WIDTH, WIDTH), BF16),
            pltpu.VMEM((PIECES, QUARTER, WIDTH), BF16),
            pltpu.VMEM((PIECES, 2, QUARTER, WIDTH), BF16),
            pltpu.VMEM((PIECES, QUARTER, WIDTH), BF16),
            pltpu.VMEM((PIECES, QUARTER, WIDTH), BF16),
            pltpu.VMEM((ROWS, WIDTH), BF16),
            pltpu.VMEM((WIDTH, 2 * WIDTH), BF16),
            pltpu.VMEM((2 * WIDTH, WIDTH), BF16),
            pltpu.SemaphoreType.DMA((MAX_COPIES,)),
            pltpu.SemaphoreType.DMA((MAX_COPIES,)),
            pltpu.SemaphoreType.DMA((6,)),
        ],
        compiler_params=pltpu.CompilerParams(
            collective_id=0, has_side_effects=True, vmem_limit_bytes=54 << 20
        ),
        cost_estimate=pl.CostEstimate(
            flops=6 * 2 * TOK * WIDTH * 2 * WIDTH, bytes_accessed=12 << 20, transcendentals=0
        ),
        name="mlp_block",
    )(tokens, w_in, w_out, gain, cotangent)
    return pl.pallas_call(
        write_out,
        out_shape=(
            jax.ShapeDtypeStruct((ROWS, WIDTH), BF16),
            jax.ShapeDtypeStruct((ROWS, WIDTH), BF16),
            jax.ShapeDtypeStruct((WIDTH, 2 * WIDTH), BF16),
            jax.ShapeDtypeStruct((2 * WIDTH, WIDTH), BF16),
        ),
        in_specs=[anywhere] * 3,
        out_specs=(anywhere,) * 4,
        scratch_shapes=[pltpu.SemaphoreType.DMA((2 + 2 * PIECES,))],
        compiler_params=pltpu.CompilerParams(vmem_limit_bytes=1 << 20),
        name="write_out",
    )(*(pltpu.with_memory_space_constraint(x, pltpu.VMEM) for x in (mixed, grad_input, pieces)))


def solution(mesh):
    in_specs = (
        P(("dp", "tok"), "hid"),
        P("hid", "tok"),
        P("tok", "hid"),
        P("hid"),
        P(("dp", "tok"), "hid"),
    )
    out_specs = (P(("dp", "tok"), "hid"), P(("dp", "tok"), "hid"), P("hid", "tok"), P("tok", "hid"))
    return jax.shard_map(shards, mesh=mesh, in_specs=in_specs, out_specs=out_specs, check_vma=False)
```

```python
import functools
import math

import jax
import jax.numpy as jnp
from jax import lax
from jax.experimental import pallas as pl
from jax.experimental.pallas import tpu as pltpu
from jax.sharding import PartitionSpec as P

D = 3072
ROWS = 128
WIDTH = 768
TOK = 1024
N_TOK = 8
N_Y = 4
QUARTER = WIDTH // N_Y
EIGHTH = QUARTER // 2
SHARE = ROWS // 2
PIECES = 4
X_LAST = (1,)
MAX_COPIES = 220
SUB = WIDTH // 2
GROUPS = ((0, 128), (128, 256), (384, 256), (640, 256), (896, 128))

norm_eps = 1e-06
GRAD_SCALE = 1.0 / math.sqrt(8192)
MESH = pl.DeviceIdType.MESH
BF16 = jnp.bfloat16
F32 = jnp.float32


def gelu_pair(pre_act):
    cdf_part = 0.5 * (1.0 + lax.erf(pre_act * (1.0 / math.sqrt(2.0))))
    dens_part = jnp.exp(-0.5 * pre_act * pre_act) * (1.0 / math.sqrt(2.0 * math.pi))
    return (pre_act * cdf_part, cdf_part + pre_act * dens_part)


def dot(left_op, right_op):
    return jnp.dot(left_op, right_op, preferred_element_type=F32)


def right_contract(left_op, right_op):
    return lax.dot_general(
        left_op, right_op, (((1,), (1,)), ((), ())), preferred_element_type=F32
    )


def row_contract(left_op, right_op):
    return lax.dot_general(
        left_op, right_op, (((0,), (0,)), ((), ())), preferred_element_type=F32
    )


def block(start, size):
    return pl.ds(start if isinstance(start, int) else pl.multiple_of(start, 16), size)


def kernel(
    tok_ref, win_ref, wout_ref, gain_ref, cot_ref,
    mixed_ref, gin_ref, pieces_ref,
    winc, woutc, xf, cf, pf, rf, pb, rb, slopes, hid, ghid,
    branch, zf, gnorm, zb, stat_out, stat_in, totals, scaled,
    dw, anti, near, qsum, far, tok_buf, win_buf, wout_buf, ssem, rsem, lsem,
):
    dp, z, h = lax.axis_index("dp"), lax.axis_index("tok"), lax.axis_index("hid")
    y, xh = dp // 2, dp % 2
    xl, c = h // 2, h % 2
    zp, zm = (dp, (z + 1) % N_TOK, h), (dp, (z + N_TOK - 1) % N_TOK, h)
    sib = (dp, z, xl * 2 + 1 - c)
    xn = (dp, z, (1 - xl) * 2 + c)
    diag = (dp, z, (1 - xl) * 2 + 1 - c)
    yp, ym = (((y + 1) % N_Y) * 2 + xh, z, h), (((y + N_Y - 1) % N_Y) * 2 + xh, z, h)
    xo = (y * 2 + 1 - xh, z, h)
    peers = (zp, zm, sib, xn, diag, yp, ym, xo)

    own_half, sib_half = c * WIDTH, (1 - c) * WIDTH
    lane_own = pl.ds(pl.multiple_of(own_half, WIDTH), WIDTH)

    barrier = pltpu.get_barrier_semaphore()
    for peer in peers:
        pl.semaphore_signal(barrier, inc=1, device_id=peer, device_id_type=MESH)

    local = [
        pltpu.make_async_copy(tok_ref, tok_buf, lsem.at[0]),
        pltpu.make_async_copy(cot_ref, cf.at[c, pl.ds(0, ROWS)], lsem.at[1]),
        pltpu.make_async_copy(wout_ref.at[lane_own, :], woutc.at[c], lsem.at[2]),
        pltpu.make_async_copy(win_ref.at[:, lane_own], winc.at[c], lsem.at[3]),
        pltpu.make_async_copy(wout_ref, wout_buf, lsem.at[4]),
        pltpu.make_async_copy(win_ref, win_buf, lsem.at[5]),
    ]
    for copy in local:
        copy.start()

    sent = []

    def send(src, dst, peer):
        i = len(sent)
        copy = pltpu.make_async_remote_copy(
            src_ref=src, dst_ref=dst, send_sem=ssem.at[i], recv_sem=rsem.at[i],
            device_id=peer, device_id_type=MESH,
        )
        copy.start()
        sent.append(copy)
        return copy

    def slot(r, lo=0, size=ROWS):
        return block(r * ROWS + lo, size)

    def ring_first(src, buf):
        return [
            (send(src, buf.at[c, slot(1)], zp),),
            (send(src, buf.at[c, slot(2)], zm),),
            send(src, buf.at[c, slot(0)], sib),
        ]

    ring = {"c": {}, "x": {}}
    sib_copies = {"c": {}, "x": {}}
    bufs = {"c": cf, "x": xf}

    def start_ring(name, src):
        up, down, across = ring_first(src, bufs[name])
        ring[name][1] = up + down
        sib_copies[name][0] = across

    def ring_wait(name, k):
        buf = bufs[name]
        for copy in ring[name][k]:
            copy.wait_recv()
        rows = block(*GROUPS[k])
        sib_copies[name][k] = send(buf.at[c, rows], buf.at[c, rows], sib)

    def ring_forward(name, k):
        buf = bufs[name]
        a, b = 2 * k - 1, 2 * k
        if k < 3:
            ring[name][k + 1] = (
                send(buf.at[c, slot(a)], buf.at[c, slot(a + 2)], zp),
                send(buf.at[c, slot(b)], buf.at[c, slot(b + 2)], zm),
            )
        else:
            lo, hi = (0, SHARE), (SHARE, SHARE)
            ring[name][4] = (
                send(buf.at[c, slot(a, *lo)], buf.at[c, slot(7, *lo)], zp),
                send(buf.at[c, slot(b, *hi)], buf.at[c, slot(7, *hi)], zm),
            )

    lanes = lax.broadcasted_iota(jnp.int32, (ROWS, ROWS), 1)

    def share_stats(i, first, second):
        stat_out[i] = jnp.where(lanes == 0, first, second).T[0:8]
        return [
            send(stat_out.at[i], stat_in.at[i, j], peer)
            for j, peer in enumerate((xn, diag, sib))
        ]

    def total_stats(i, copies):
        for copy in copies:
            copy.wait_recv()
        total = (stat_out[i] + stat_in[i, 2]) + (stat_in[i, 0] + stat_in[i, 1])
        columns = jnp.concatenate([total] * (ROWS // 8), axis=0).T
        return columns[:, 0:1], columns[:, 1:2]

    local[0].wait()
    tok_float = tok_buf[...].astype(F32)
    tok_sum = jnp.sum(tok_float, axis=1, keepdims=True)
    tok_squares = jnp.sum(tok_float * tok_float, axis=1, keepdims=True)
    pl.semaphore_wait(barrier, len(peers))
    stats = share_stats(0, tok_sum, tok_squares)
    local[1].wait()
    start_ring("c", cf.at[c, slot(0)])
    weight_copies = {}
    for u in range(2):
        theirs = pl.ds(pl.multiple_of(sib_half + u * SUB, SUB), SUB)
        here = pl.ds(u * SUB, SUB)
        weight_copies["out", u] = send(wout_ref.at[theirs, :], woutc.at[c, here, :], sib)
        weight_copies["in", u] = send(win_ref.at[:, theirs], winc.at[c, :, here], sib)

    def sub(part):
        return pl.ds(part * SUB, SUB)

    arrived = set()

    def arrive(key, *waits):
        if key not in arrived:
            arrived.add(key)
            for wait in waits:
                wait()

    partial_copies = {"f": {}, "b": {}}
    share_copies = {"f": {}, "b": {}}
    whole_copies = {"f": {}, "b": {}}

    def send_partial(name, part, landing, g, u):
        start, count = GROUPS[g]
        half = count // 2
        partial_copies[name][g, u] = send(
            part.at[block(start + (1 - xl) * half, half), sub(u)],
            landing.at[block(start // 2, half), sub(u)],
            xn,
        )

    def send_share(name, buf, g, u):
        start, count = GROUPS[g]
        half = count // 2
        mine = buf.at[c, block(start + xl * half, half), sub(u)]
        share_copies[name][g, u] = send(mine, mine, xn)

    def f1(g, u):
        arrive("win", local[3].wait)
        arrive(("in", u), weight_copies["in", u].wait_recv)
        arrive(("x", g), sib_copies["x"][g].wait_recv)
        rows, cols = block(*GROUPS[g]), sub(u)
        total = dot(xf[0, rows], winc[0, :, cols]) + dot(xf[1, rows], winc[1, :, cols])
        pf[rows, cols] = total.astype(BF16)
        send_partial("f", pf, rf, g, u)

    def b1(g, u):
        arrive("wout", local[2].wait)
        arrive(("out", u), weight_copies["out", u].wait_recv)
        arrive(("c", g), sib_copies["c"][g].wait_recv)
        rows, cols = block(*GROUPS[g]), sub(u)
        total = right_contract(cf[0, rows], woutc[0, cols, :])
        total += right_contract(cf[1, rows], woutc[1, cols, :])
        pb[rows, cols] = total.astype(BF16)
        send_partial("b", pb, rb, g, u)

    def f2(g, u):
        partial_copies["f"][g, u].wait_recv()
        start, count = GROUPS[g]
        mine, landed = start + xl * (count // 2), start // 2

        def tile(n, carry):
            k = n * 32
            pre_act = pf[block(mine + k, 32), sub(u)].astype(F32)
            pre_act += rf[block(landed + k, 32), sub(u)].astype(F32)
            act, slope = gelu_pair(pre_act)
            slopes[block(landed + k, 32), sub(u)] = slope
            hid[c, block(mine + k, 32), sub(u)] = act.astype(BF16)
            return carry

        lax.fori_loop(0, count // 64, tile, 0)
        send_share("f", hid, g, u)

    def b2(g, u):
        partial_copies["b"][g, u].wait_recv()
        start, count = GROUPS[g]
        mine, landed = start + xl * (count // 2), start // 2

        def tile(n, carry):
            k = n * 32
            grad = pb[block(mine + k, 32), sub(u)].astype(F32)
            grad += rb[block(landed + k, 32), sub(u)].astype(F32)
            grad *= slopes[block(landed + k, 32), sub(u)]
            ghid[c, block(mine + k, 32), sub(u)] = grad.astype(BF16)
            return carry

        lax.fori_loop(0, count // 64, tile, 0)
        send_share("b", ghid, g, u)

    def third(name, buf, g, u):
        share_copies[name][g, u].wait_recv()
        whole = buf.at[c, block(*GROUPS[g]), sub(u)]
        whole_copies[name][g, u] = send(whole, whole, sib)

    def f3(g, u):
        third("f", hid, g, u)

    def b3(g, u):
        third("b", ghid, g, u)

    def whole_wait(name, u):
        waits = [whole_copies[name][g, u].wait_recv for g in range(len(GROUPS))]
        arrive((name, "whole", u), *waits)

    def product_rows(src, dst, i, transposed):
        for u in range(2):
            whole_wait("b" if transposed else "f", u)
        rows = block(i * 256, 256)
        if transposed:
            arrive("win_buf", local[5].wait)
            total = right_contract(src[0, rows], win_buf[:, 0:WIDTH])
            total += right_contract(src[1, rows], win_buf[:, WIDTH : 2 * WIDTH])
        else:
            arrive("wout_buf", local[4].wait)
            total = dot(src[0, rows], wout_buf[0:WIDTH, :])
            total += dot(src[1, rows], wout_buf[WIDTH : 2 * WIDTH, :])
        dst[rows, :] = total.astype(BF16)

    def add_rows(dst, at, src, rows, count):
        def tile(n, carry):
            here = block(at + n * 16, 16)
            there = block(rows + n * 16, 16)
            dst[here, :] = (dst[here, :].astype(F32) + src[there, :].astype(F32)).astype(BF16)
            return carry

        lax.fori_loop(0, count // 16, tile, 0)

    back = {"f": {}, "b": {}}

    def ring_back(name, part, landing, k):
        if k == 4:
            back[name][4] = (
                send(part.at[slot(7, 0, SHARE)], landing.at[slot(5, 0, SHARE)], zm),
                send(part.at[slot(7, SHARE, SHARE)], landing.at[slot(6, SHARE, SHARE)], zp),
            )
            return
        a, b = 2 * k - 1, 2 * k
        for copy in back[name][k + 1]:
            copy.wait_recv()
        if k == 3:
            add_rows(part, a * ROWS, landing, a * ROWS, SHARE)
            add_rows(part, b * ROWS + SHARE, landing, b * ROWS + SHARE, SHARE)
        else:
            add_rows(part, a * ROWS, landing, a * ROWS, ROWS)
            add_rows(part, b * ROWS, landing, b * ROWS, ROWS)
        to_a, to_b = (0, 7) if k == 1 else (a - 2, b - 2)
        back[name][k] = (
            send(part.at[slot(a)], landing.at[slot(to_a)], zm),
            send(part.at[slot(b)], landing.at[slot(to_b)], zp),
        )

    def ring_total(name, part, landing):
        for copy in back[name][1]:
            copy.wait_recv()
        total = part[slot(0), :].astype(F32) + landing[slot(0), :].astype(F32)
        return total + landing[slot(7), :].astype(F32)

    qa, qb, qo = (y + 1) % N_Y, (y + N_Y - 1) % N_Y, (y + 2) % N_Y

    def weight_product(p):
        cols = sub(p % 2)
        for core in range(2):
            half = sub(core)
            if p < 2:
                total = row_contract(hid[core, :, cols], cf[c])
                dw[p, half, :] = (total * GRAD_SCALE).astype(BF16)
            else:
                total = row_contract(xf[c], ghid[core, :, cols])
                dw[p, :, half] = (total * GRAD_SCALE).astype(BF16)

    first_hop, second_hop, far_copies, spread, spread_on, across = {}, {}, {}, {}, {}, {}
    low, high = block(0, EIGHTH), block(EIGHTH, EIGHTH)

    def r1(p):
        part = dw.at[p]
        first_hop[p] = (
            send(part.at[block(qo * QUARTER, EIGHTH)], anti.at[p, low], yp),
            send(part.at[block(qo * QUARTER + EIGHTH, EIGHTH)], anti.at[p, high], ym),
        )
        second_hop[p] = (
            send(part.at[block(qa * QUARTER + EIGHTH, EIGHTH)], near.at[p, 0, high], yp),
            send(part.at[block(qb * QUARTER, EIGHTH)], near.at[p, 1, low], ym),
        )

    def r2(p):
        part = dw.at[p]
        for copy in first_hop[p]:
            copy.wait_recv()
        add_rows(part, qa * QUARTER, anti.at[p], 0, EIGHTH)
        add_rows(part, qb * QUARTER + EIGHTH, anti.at[p], EIGHTH, EIGHTH)
        second_hop[p] += (
            send(part.at[block(qa * QUARTER, EIGHTH)], near.at[p, 0, low], yp),
            send(part.at[block(qb * QUARTER + EIGHTH, EIGHTH)], near.at[p, 1, high], ym),
        )

    def r3(p):
        for copy in second_hop[p]:
            copy.wait_recv()

        def tile(n, carry):
            rows = block(n * 16, 16)
            total = dw[p, block(y * QUARTER + n * 16, 16), :].astype(F32)
            total += near[p, 0, rows, :].astype(F32) + near[p, 1, rows, :].astype(F32)
            qsum[p, rows, :] = total.astype(BF16)
            return carry

        lax.fori_loop(0, QUARTER // 16, tile, 0)
        if p in X_LAST:
            theirs = block((1 - xh) * EIGHTH, EIGHTH)
            far_copies[p] = send(qsum.at[p, theirs], far.at[p, low], xo)
        else:
            far_copies[p] = send(qsum.at[p], far.at[p], xo)

    def out_at(p, start, size):
        return pieces_ref.at[p, block(start, size)]

    def r4(p):
        far_copies[p].wait_recv()
        mine, count = (xh * EIGHTH, EIGHTH) if p in X_LAST else (0, QUARTER)

        def tile(n, carry):
            total = qsum[p, block(mine + n * 16, 16), :].astype(F32)
            total += far[p, block(n * 16, 16), :].astype(F32)
            pieces_ref[p, block(y * QUARTER + mine + n * 16, 16), :] = total.astype(BF16)
            return carry

        lax.fori_loop(0, count // 16, tile, 0)
        own = out_at(p, y * QUARTER + mine, count)
        spread[p] = (send(own, own, yp), send(own, own, ym))
        if p in X_LAST:
            across[p] = (send(own, own, xo),)

    def r5(p):
        for copy in spread[p]:
            copy.wait_recv()
        mine, half = (xh * EIGHTH, EIGHTH // 2) if p in X_LAST else (0, EIGHTH)
        behind = out_at(p, qb * QUARTER + mine, half)
        ahead = out_at(p, qa * QUARTER + mine + half, half)
        spread_on[p] = (send(behind, behind, yp), send(ahead, ahead, ym))
        if p in X_LAST:
            for q in (qb, qa):
                whole = out_at(p, q * QUARTER + mine, EIGHTH)
                across[p] += (send(whole, whole, xo),)

    def r6(p):
        for copy in spread_on[p]:
            copy.wait_recv()
        if p in X_LAST:
            whole = out_at(p, qo * QUARTER + xh * EIGHTH, EIGHTH)
            across[p] += (send(whole, whole, xo),)

    def r7(p):
        for copy in across[p]:
            copy.wait_recv()

    state = {}

    def normalize():
        row_sum, square_sum = total_stats(0, stats)
        row_mean = row_sum / D
        row_rstd = lax.rsqrt(square_sum / D - row_mean * row_mean + norm_eps)
        totals[...] = jnp.where(lanes == 0, row_mean, row_rstd)
        centred = (tok_float - row_mean) * row_rstd
        xf[c, slot(0)] = (centred * gain_ref[...][None, :]).astype(BF16)
        start_ring("x", xf.at[c, slot(0)])

    def blk(name, i):
        if name == "f":
            product_rows(hid, branch, i, False)
        else:
            product_rows(ghid, gnorm, i, True)

    def back_step(name, k):
        if name == "f":
            ring_back(name, branch, zf, k)
        else:
            ring_back(name, gnorm, zb, k)

    def finish_out():
        mixed_ref[...] = (
            tok_buf[...].astype(F32) + ring_total("f", branch, zf)
        ).astype(BF16)

    def centred_rows():
        row_mean, row_rstd = totals[:, 0:1], totals[:, 1:2]
        return (tok_buf[...].astype(F32) - row_mean) * row_rstd, row_rstd

    def share_grad():
        grad_scaled = ring_total("b", gnorm, zb) * gain_ref[...][None, :]
        scaled[...] = grad_scaled
        centred, _ = centred_rows()
        state["grad"] = share_stats(
            1,
            jnp.sum(grad_scaled, axis=1, keepdims=True),
            jnp.sum(grad_scaled * centred, axis=1, keepdims=True),
        )

    def finish_grad():
        first_sum, second_sum = total_stats(1, state["grad"])
        centred, row_rstd = centred_rows()
        gin_ref[...] = (
            cf[c, slot(0)].astype(F32)
            + row_rstd * (scaled[...] - first_sum / D - centred * (second_sum / D))
        ).astype(BF16)

    def product(p):
        whole_wait("f" if p < 2 else "b", p % 2)
        weight_product(p)
        r1(p)

    schedule = (
        (b1, 0, 0), (normalize,), (b1, 0, 1), (ring_wait, "c", 1), (f1, 0, 0), (f1, 0, 1), (b1, 1, 0),
        (ring_wait, "x", 1), (ring_forward, "x", 1), (f2, 0, 1), (f2, 0, 0), (b2, 0, 0), (f1, 1, 0),
        (f1, 1, 1), (ring_wait, "x", 2), (ring_forward, "x", 2), (f1, 2, 1), (ring_forward, "c", 1),
        (f1, 2, 0), (f2, 1, 0), (f2, 2, 1), (ring_wait, "x", 3), (b3, 0, 0), (f1, 3, 0), (f1, 3, 1),
        (ring_forward, "x", 3), (ring_wait, "c", 2), (ring_forward, "c", 2), (f3, 0, 1), (f2, 2, 0),
        (f3, 1, 0), (ring_wait, "x", 4), (f1, 4, 0), (f2, 3, 0), (ring_wait, "c", 3), (f2, 4, 0),
        (ring_forward, "c", 3), (f2, 3, 1), (f1, 4, 1), (f3, 2, 0), (f3, 3, 0), (f3, 0, 0), (b1, 2, 0),
        (f3, 4, 0), (ring_wait, "c", 4), (product, 0), (f3, 3, 1), (f2, 4, 1), (b1, 4, 0), (f3, 2, 1),
        (b2, 1, 0), (f3, 4, 1), (f2, 1, 1), (b1, 3, 0), (b2, 2, 0), (b1, 2, 1), (r2, 0), (f3, 1, 1),
        (product, 1), (b2, 4, 0), (b2, 3, 0), (r3, 0), (blk, "f", 0), (b3, 2, 0), (b3, 1, 0), (b1, 1, 1),
        (b3, 4, 0), (blk, "f", 2), (b2, 2, 1), (r2, 1), (blk, "f", 3), (b3, 3, 0), (product, 2), (b1, 3, 1),
        (b1, 4, 1), (blk, "f", 1), (r4, 0), (b2, 1, 1), (b2, 3, 1), (back_step, "f", 4), (b2, 0, 1),
        (b2, 4, 1), (r2, 2), (b3, 3, 1), (r5, 0), (b3, 1, 1), (b3, 2, 1), (r3, 1), (b3, 0, 1), (b3, 4, 1),
        (product, 3), (back_step, "f", 3), (blk, "b", 3), (r3, 2), (r2, 3), (back_step, "b", 4), (r4, 1),
        (blk, "b", 2), (back_step, "f", 2), (back_step, "b", 3), (r4, 2), (blk, "b", 0), (r3, 3),
        (blk, "b", 1), (back_step, "b", 2), (r5, 1), (r4, 3), (r6, 0), (back_step, "b", 1),
        (back_step, "f", 1), (r5, 2), (r6, 1), (share_grad,), (r5, 3), (finish_grad,), (finish_out,), (r6, 2),
        (r7, 1), (r6, 3),
    )
    for step, *where in schedule:
        step(*where)
    for copy in sent:
        copy.wait_send()


def write_out(mixed_in, gin_in, pieces, mixed_ref, gin_ref, gwin_ref, gwout_ref, sems):
    pairs = [(mixed_in, mixed_ref), (gin_in, gin_ref)]
    for p in range(PIECES):
        for core in range(2):
            half = pl.ds(core * SUB, SUB)
            place = pl.ds(core * WIDTH + (p % 2) * SUB, SUB)
            if p < 2:
                pairs.append((pieces.at[p, half, :], gwout_ref.at[place, :]))
            else:
                pairs.append((pieces.at[p, :, half], gwin_ref.at[:, place]))
    copies = [
        pltpu.make_async_copy(src, dst, sems.at[i]) for i, (src, dst) in enumerate(pairs)
    ]
    for copy in copies:
        copy.start()
    for copy in copies:
        copy.wait()


def shards(tokens, w_in, w_out, gain, cotangent):
    vmem = pl.BlockSpec(memory_space=pltpu.VMEM)
    anywhere = pl.BlockSpec(memory_space=pl.ANY)
    mixed, grad_input, pieces = pl.pallas_call(
        kernel,
        out_shape=(
            pltpu.VMEM((ROWS, WIDTH), BF16),
            pltpu.VMEM((ROWS, WIDTH), BF16),
            pltpu.VMEM((PIECES, WIDTH, WIDTH), BF16),
        ),
        in_specs=[anywhere, anywhere, anywhere, vmem, anywhere],
        out_specs=(vmem,) * 3,
        scratch_shapes=[
            pltpu.VMEM((2, WIDTH, WIDTH), BF16),
            pltpu.VMEM((2, WIDTH, WIDTH), BF16),
            pltpu.VMEM((2, TOK, WIDTH), BF16),
            pltpu.VMEM((2, TOK, WIDTH), BF16),
            pltpu.VMEM((TOK, WIDTH), BF16),
            pltpu.VMEM((TOK // 2, WIDTH), BF16),
            pltpu.VMEM((TOK, WIDTH), BF16),
            pltpu.VMEM((TOK // 2, WIDTH), BF16),
            pltpu.VMEM((TOK // 2, WIDTH), F32),
            pltpu.VMEM((2, TOK, WIDTH), BF16),
            pltpu.VMEM((2, TOK, WIDTH), BF16),
            pltpu.VMEM((TOK, WIDTH), BF16),
            pltpu.VMEM((TOK, WIDTH), BF16),
            pltpu.VMEM((TOK, WIDTH), BF16),
            pltpu.VMEM((TOK, WIDTH), BF16),
            pltpu.VMEM((2, 8, ROWS), F32),
            pltpu.VMEM((2, 3, 8, ROWS), F32),
            pltpu.VMEM((ROWS, ROWS), F32),
            pltpu.VMEM((ROWS, WIDTH), F32),
            pltpu.VMEM((PIECES, WIDTH, WIDTH), BF16),
            pltpu.VMEM((PIECES, QUARTER, WIDTH), BF16),
            pltpu.VMEM((PIECES, 2, QUARTER, WIDTH), BF16),
            pltpu.VMEM((PIECES, QUARTER, WIDTH), BF16),
            pltpu.VMEM((PIECES, QUARTER, WIDTH), BF16),
            pltpu.VMEM((ROWS, WIDTH), BF16),
            pltpu.VMEM((WIDTH, 2 * WIDTH), BF16),
            pltpu.VMEM((2 * WIDTH, WIDTH), BF16),
            pltpu.SemaphoreType.DMA((MAX_COPIES,)),
            pltpu.SemaphoreType.DMA((MAX_COPIES,)),
            pltpu.SemaphoreType.DMA((6,)),
        ],
        compiler_params=pltpu.CompilerParams(
            collective_id=0, has_side_effects=True, vmem_limit_bytes=54 << 20
        ),
        cost_estimate=pl.CostEstimate(
            flops=6 * 2 * TOK * WIDTH * 2 * WIDTH, bytes_accessed=12 << 20, transcendentals=0
        ),
        name="mlp_block",
    )(tokens, w_in, w_out, gain, cotangent)
    return pl.pallas_call(
        write_out,
        out_shape=(
            jax.ShapeDtypeStruct((ROWS, WIDTH), BF16),
            jax.ShapeDtypeStruct((ROWS, WIDTH), BF16),
            jax.ShapeDtypeStruct((WIDTH, 2 * WIDTH), BF16),
            jax.ShapeDtypeStruct((2 * WIDTH, WIDTH), BF16),
        ),
        in_specs=[anywhere] * 3,
        out_specs=(anywhere,) * 4,
        scratch_shapes=[pltpu.SemaphoreType.DMA((2 + 2 * PIECES,))],
        compiler_params=pltpu.CompilerParams(vmem_limit_bytes=1 << 20),
        name="write_out",
    )(*(pltpu.with_memory_space_constraint(x, pltpu.VMEM) for x in (mixed, grad_input, pieces)))


def solution(mesh):
    in_specs = (
        P(("dp", "tok"), "hid"),
        P("hid", "tok"),
        P("tok", "hid"),
        P("hid"),
        P(("dp", "tok"), "hid"),
    )
    out_specs = (P(("dp", "tok"), "hid"), P(("dp", "tok"), "hid"), P("hid", "tok"), P("tok", "hid"))
    return jax.shard_map(shards, mesh=mesh, in_specs=in_specs, out_specs=out_specs, check_vma=False)
```

```python
import functools
import math

import jax
import jax.numpy as jnp
from jax import lax
from jax.experimental import pallas as pl
from jax.experimental.pallas import tpu as pltpu
from jax.sharding import PartitionSpec as P

D = 3072
ROWS = 128
WIDTH = 768
TOK = 1024
N_TOK = 8
N_Y = 4
HALF = WIDTH // 2
QUARTER = HALF // N_Y
EIGHTH = QUARTER // 2
SHARE = ROWS // 2
PIECES = 8
X_LAST = (2, 3)
MAX_COPIES = 256
SUB = WIDTH // 2
GROUPS = ((0, 128), (128, 256), (384, 256), (640, 256), (896, 128))

norm_eps = 1e-06
GRAD_SCALE = 1.0 / math.sqrt(8192)
MESH = pl.DeviceIdType.MESH
BF16 = jnp.bfloat16
F32 = jnp.float32


def gelu_pair(pre_act):
    cdf_part = 0.5 * (1.0 + lax.erf(pre_act * (1.0 / math.sqrt(2.0))))
    dens_part = jnp.exp(-0.5 * pre_act * pre_act) * (1.0 / math.sqrt(2.0 * math.pi))
    return (pre_act * cdf_part, cdf_part + pre_act * dens_part)


def dot(left_op, right_op):
    return jnp.dot(left_op, right_op, preferred_element_type=F32)


def right_contract(left_op, right_op):
    return lax.dot_general(
        left_op, right_op, (((1,), (1,)), ((), ())), preferred_element_type=F32
    )


def row_contract(left_op, right_op):
    return lax.dot_general(
        left_op, right_op, (((0,), (0,)), ((), ())), preferred_element_type=F32
    )


def block(start, size):
    return pl.ds(start if isinstance(start, int) else pl.multiple_of(start, 16), size)


def kernel(
    tok_ref, win_ref, wout_ref, gain_ref, cot_ref,
    mixed_ref, gin_ref, pieces_ref,
    winc, woutc, xf, cf, pf, rf, pb, rb, slopes, hid, ghid,
    branch, zf, gnorm, zb, stat_out, stat_in, totals, scaled,
    dw, anti, near, qsum, far, tok_buf, win_buf, wout_buf, ssem, rsem, lsem,
):
    dp, z, h = lax.axis_index("dp"), lax.axis_index("tok"), lax.axis_index("hid")
    y, xh = dp // 2, dp % 2
    xl, c = h // 2, h % 2
    zp, zm = (dp, (z + 1) % N_TOK, h), (dp, (z + N_TOK - 1) % N_TOK, h)
    sib = (dp, z, xl * 2 + 1 - c)
    xn = (dp, z, (1 - xl) * 2 + c)
    diag = (dp, z, (1 - xl) * 2 + 1 - c)
    yp, ym = (((y + 1) % N_Y) * 2 + xh, z, h), (((y + N_Y - 1) % N_Y) * 2 + xh, z, h)
    xo = (y * 2 + 1 - xh, z, h)
    peers = (zp, zm, sib, xn, diag, yp, ym, xo)

    own_half, sib_half = c * WIDTH, (1 - c) * WIDTH
    lane_own = pl.ds(pl.multiple_of(own_half, WIDTH), WIDTH)

    barrier = pltpu.get_barrier_semaphore()
    for peer in peers:
        pl.semaphore_signal(barrier, inc=1, device_id=peer, device_id_type=MESH)

    local = [
        pltpu.make_async_copy(tok_ref, tok_buf, lsem.at[0]),
        pltpu.make_async_copy(cot_ref, cf.at[c, pl.ds(0, ROWS)], lsem.at[1]),
        pltpu.make_async_copy(wout_ref.at[lane_own, :], woutc.at[c], lsem.at[2]),
        pltpu.make_async_copy(win_ref.at[:, lane_own], winc.at[c], lsem.at[3]),
        pltpu.make_async_copy(wout_ref, wout_buf, lsem.at[4]),
        pltpu.make_async_copy(win_ref, win_buf, lsem.at[5]),
    ]
    for copy in local:
        copy.start()

    sent = []

    def send(src, dst, peer):
        i = len(sent)
        copy = pltpu.make_async_remote_copy(
            src_ref=src, dst_ref=dst, send_sem=ssem.at[i], recv_sem=rsem.at[i],
            device_id=peer, device_id_type=MESH,
        )
        copy.start()
        sent.append(copy)
        return copy

    def slot(r, lo=0, size=ROWS):
        return block(r * ROWS + lo, size)

    def ring_first(src, buf):
        return [
            (send(src, buf.at[c, slot(1)], zp),),
            (send(src, buf.at[c, slot(2)], zm),),
            send(src, buf.at[c, slot(0)], sib),
        ]

    ring = {"c": {}, "x": {}}
    sib_copies = {"c": {}, "x": {}}
    bufs = {"c": cf, "x": xf}

    def start_ring(name, src):
        up, down, across = ring_first(src, bufs[name])
        ring[name][1] = up + down
        sib_copies[name][0] = across

    def ring_wait(name, k):
        buf = bufs[name]
        for copy in ring[name][k]:
            copy.wait_recv()
        rows = block(*GROUPS[k])
        sib_copies[name][k] = send(buf.at[c, rows], buf.at[c, rows], sib)

    def ring_forward(name, k):
        buf = bufs[name]
        a, b = 2 * k - 1, 2 * k
        if k < 3:
            ring[name][k + 1] = (
                send(buf.at[c, slot(a)], buf.at[c, slot(a + 2)], zp),
                send(buf.at[c, slot(b)], buf.at[c, slot(b + 2)], zm),
            )
        else:
            lo, hi = (0, SHARE), (SHARE, SHARE)
            ring[name][4] = (
                send(buf.at[c, slot(a, *lo)], buf.at[c, slot(7, *lo)], zp),
                send(buf.at[c, slot(b, *hi)], buf.at[c, slot(7, *hi)], zm),
            )

    lanes = lax.broadcasted_iota(jnp.int32, (ROWS, ROWS), 1)

    def share_stats(i, first, second):
        stat_out[i] = jnp.where(lanes == 0, first, second).T[0:8]
        return [
            send(stat_out.at[i], stat_in.at[i, j], peer)
            for j, peer in enumerate((xn, diag, sib))
        ]

    def total_stats(i, copies):
        for copy in copies:
            copy.wait_recv()
        total = (stat_out[i] + stat_in[i, 2]) + (stat_in[i, 0] + stat_in[i, 1])
        columns = jnp.concatenate([total] * (ROWS // 8), axis=0).T
        return columns[:, 0:1], columns[:, 1:2]

    local[0].wait()
    tok_float = tok_buf[...].astype(F32)
    tok_sum = jnp.sum(tok_float, axis=1, keepdims=True)
    tok_squares = jnp.sum(tok_float * tok_float, axis=1, keepdims=True)
    pl.semaphore_wait(barrier, len(peers))
    stats = share_stats(0, tok_sum, tok_squares)
    local[1].wait()
    start_ring("c", cf.at[c, slot(0)])
    weight_copies = {}
    for u in range(2):
        theirs = pl.ds(pl.multiple_of(sib_half + u * SUB, SUB), SUB)
        here = pl.ds(u * SUB, SUB)
        weight_copies["out", u] = send(wout_ref.at[theirs, :], woutc.at[c, here, :], sib)
        weight_copies["in", u] = send(win_ref.at[:, theirs], winc.at[c, :, here], sib)

    def sub(part):
        return pl.ds(part * SUB, SUB)

    arrived = set()

    def arrive(key, *waits):
        if key not in arrived:
            arrived.add(key)
            for wait in waits:
                wait()

    partial_copies = {"f": {}, "b": {}}
    share_copies = {"f": {}, "b": {}}
    whole_copies = {"f": {}, "b": {}}

    def send_partial(name, part, landing, g, u):
        start, count = GROUPS[g]
        half = count // 2
        partial_copies[name][g, u] = send(
            part.at[block(start + (1 - xl) * half, half), sub(u)],
            landing.at[block(start // 2, half), sub(u)],
            xn,
        )

    def send_share(name, buf, g, u):
        start, count = GROUPS[g]
        half = count // 2
        mine = buf.at[c, block(start + xl * half, half), sub(u)]
        share_copies[name][g, u] = send(mine, mine, xn)

    def f1(g, u):
        arrive("win", local[3].wait)
        arrive(("in", u), weight_copies["in", u].wait_recv)
        arrive(("x", g), sib_copies["x"][g].wait_recv)
        rows, cols = block(*GROUPS[g]), sub(u)
        total = dot(xf[0, rows], winc[0, :, cols]) + dot(xf[1, rows], winc[1, :, cols])
        pf[rows, cols] = total.astype(BF16)
        send_partial("f", pf, rf, g, u)

    def b1(g, u):
        arrive("wout", local[2].wait)
        arrive(("out", u), weight_copies["out", u].wait_recv)
        arrive(("c", g), sib_copies["c"][g].wait_recv)
        rows, cols = block(*GROUPS[g]), sub(u)
        total = right_contract(cf[0, rows], woutc[0, cols, :])
        total += right_contract(cf[1, rows], woutc[1, cols, :])
        pb[rows, cols] = total.astype(BF16)
        send_partial("b", pb, rb, g, u)

    def f2(g, u):
        partial_copies["f"][g, u].wait_recv()
        start, count = GROUPS[g]
        mine, landed = start + xl * (count // 2), start // 2

        def tile(n, carry):
            k = n * 32
            pre_act = pf[block(mine + k, 32), sub(u)].astype(F32)
            pre_act += rf[block(landed + k, 32), sub(u)].astype(F32)
            act, slope = gelu_pair(pre_act)
            slopes[block(landed + k, 32), sub(u)] = slope
            hid[c, block(mine + k, 32), sub(u)] = act.astype(BF16)
            return carry

        lax.fori_loop(0, count // 64, tile, 0)
        send_share("f", hid, g, u)

    def b2(g, u):
        partial_copies["b"][g, u].wait_recv()
        start, count = GROUPS[g]
        mine, landed = start + xl * (count // 2), start // 2

        def tile(n, carry):
            k = n * 32
            grad = pb[block(mine + k, 32), sub(u)].astype(F32)
            grad += rb[block(landed + k, 32), sub(u)].astype(F32)
            grad *= slopes[block(landed + k, 32), sub(u)]
            ghid[c, block(mine + k, 32), sub(u)] = grad.astype(BF16)
            return carry

        lax.fori_loop(0, count // 64, tile, 0)
        send_share("b", ghid, g, u)

    def third(name, buf, g, u):
        share_copies[name][g, u].wait_recv()
        whole = buf.at[c, block(*GROUPS[g]), sub(u)]
        whole_copies[name][g, u] = send(whole, whole, sib)

    def f3(g, u):
        third("f", hid, g, u)

    def b3(g, u):
        third("b", ghid, g, u)

    def whole_wait(name, u):
        waits = [whole_copies[name][g, u].wait_recv for g in range(len(GROUPS))]
        arrive((name, "whole", u), *waits)

    def product_rows(src, dst, i, transposed):
        for u in range(2):
            whole_wait("b" if transposed else "f", u)
        rows = block(i * 256, 256)
        if transposed:
            arrive("win_buf", local[5].wait)
            total = right_contract(src[0, rows], win_buf[:, 0:WIDTH])
            total += right_contract(src[1, rows], win_buf[:, WIDTH : 2 * WIDTH])
        else:
            arrive("wout_buf", local[4].wait)
            total = dot(src[0, rows], wout_buf[0:WIDTH, :])
            total += dot(src[1, rows], wout_buf[WIDTH : 2 * WIDTH, :])
        dst[rows, :] = total.astype(BF16)

    def add_rows(dst, at, src, rows, count):
        def tile(n, carry):
            here = block(at + n * 16, 16)
            there = block(rows + n * 16, 16)
            dst[here, :] = (dst[here, :].astype(F32) + src[there, :].astype(F32)).astype(BF16)
            return carry

        lax.fori_loop(0, count // 16, tile, 0)

    back = {"f": {}, "b": {}}

    def ring_back(name, part, landing, k):
        if k == 4:
            back[name][4] = (
                send(part.at[slot(7, 0, SHARE)], landing.at[slot(5, 0, SHARE)], zm),
                send(part.at[slot(7, SHARE, SHARE)], landing.at[slot(6, SHARE, SHARE)], zp),
            )
            return
        a, b = 2 * k - 1, 2 * k
        for copy in back[name][k + 1]:
            copy.wait_recv()
        if k == 3:
            add_rows(part, a * ROWS, landing, a * ROWS, SHARE)
            add_rows(part, b * ROWS + SHARE, landing, b * ROWS + SHARE, SHARE)
        else:
            add_rows(part, a * ROWS, landing, a * ROWS, ROWS)
            add_rows(part, b * ROWS, landing, b * ROWS, ROWS)
        to_a, to_b = (0, 7) if k == 1 else (a - 2, b - 2)
        back[name][k] = (
            send(part.at[slot(a)], landing.at[slot(to_a)], zm),
            send(part.at[slot(b)], landing.at[slot(to_b)], zp),
        )

    def ring_total(name, part, landing):
        for copy in back[name][1]:
            copy.wait_recv()
        total = part[slot(0), :].astype(F32) + landing[slot(0), :].astype(F32)
        return total + landing[slot(7), :].astype(F32)

    qa, qb, qo = (y + 1) % N_Y, (y + N_Y - 1) % N_Y, (y + 2) % N_Y

    def weight_product(p):
        cols = sub(p % 2)
        for core in range(2):
            half = sub(core)
            if p < 2:
                total = row_contract(hid[core, :, cols], cf[c])
                dw[2 * p + core] = (total * GRAD_SCALE).astype(BF16)
            else:
                total = (row_contract(xf[c], ghid[core, :, cols]) * GRAD_SCALE).astype(BF16)
                dw[2 * p, :, half] = total[0:HALF]
                dw[2 * p + 1, :, half] = total[HALF:WIDTH]

    first_hop, second_hop, far_copies, spread, spread_on, across = {}, {}, {}, {}, {}, {}
    low, high = block(0, EIGHTH), block(EIGHTH, EIGHTH)

    def r1(p):
        part = dw.at[p]
        first_hop[p] = (
            send(part.at[block(qo * QUARTER, EIGHTH)], anti.at[p, low], yp),
            send(part.at[block(qo * QUARTER + EIGHTH, EIGHTH)], anti.at[p, high], ym),
        )
        second_hop[p] = (
            send(part.at[block(qa * QUARTER + EIGHTH, EIGHTH)], near.at[p, 0, high], yp),
            send(part.at[block(qb * QUARTER, EIGHTH)], near.at[p, 1, low], ym),
        )

    def r2(p):
        part = dw.at[p]
        for copy in first_hop[p]:
            copy.wait_recv()
        add_rows(part, qa * QUARTER, anti.at[p], 0, EIGHTH)
        add_rows(part, qb * QUARTER + EIGHTH, anti.at[p], EIGHTH, EIGHTH)
        second_hop[p] += (
            send(part.at[block(qa * QUARTER, EIGHTH)], near.at[p, 0, low], yp),
            send(part.at[block(qb * QUARTER + EIGHTH, EIGHTH)], near.at[p, 1, high], ym),
        )

    def r3(p):
        for copy in second_hop[p]:
            copy.wait_recv()

        def tile(n, carry):
            rows = block(n * 16, 16)
            total = dw[p, block(y * QUARTER + n * 16, 16), :].astype(F32)
            total += near[p, 0, rows, :].astype(F32) + near[p, 1, rows, :].astype(F32)
            qsum[p, rows, :] = total.astype(BF16)
            return carry

        lax.fori_loop(0, QUARTER // 16, tile, 0)
        if p in X_LAST:
            theirs = block((1 - xh) * EIGHTH, EIGHTH)
            far_copies[p] = send(qsum.at[p, theirs], far.at[p, low], xo)
        else:
            far_copies[p] = send(qsum.at[p], far.at[p], xo)

    def out_at(p, start, size):
        return pieces_ref.at[p, block(start, size)]

    def r4(p):
        far_copies[p].wait_recv()
        mine, count = (xh * EIGHTH, EIGHTH) if p in X_LAST else (0, QUARTER)

        def tile(n, carry):
            total = qsum[p, block(mine + n * 16, 16), :].astype(F32)
            total += far[p, block(n * 16, 16), :].astype(F32)
            pieces_ref[p, block(y * QUARTER + mine + n * 16, 16), :] = total.astype(BF16)
            return carry

        lax.fori_loop(0, count // 16, tile, 0)
        own = out_at(p, y * QUARTER + mine, count)
        spread[p] = (send(own, own, yp), send(own, own, ym))
        if p in X_LAST:
            across[p] = (send(own, own, xo),)

    def r5(p):
        for copy in spread[p]:
            copy.wait_recv()
        mine, half, rest = (xh * EIGHTH, 32, 16) if p in X_LAST else (0, EIGHTH, EIGHTH)
        behind = out_at(p, qb * QUARTER + mine, half)
        ahead = out_at(p, qa * QUARTER + mine + half, rest)
        spread_on[p] = (send(behind, behind, yp), send(ahead, ahead, ym))
        if p in X_LAST:
            for q in (qb, qa):
                whole = out_at(p, q * QUARTER + mine, EIGHTH)
                across[p] += (send(whole, whole, xo),)

    def r6(p):
        for copy in spread_on[p]:
            copy.wait_recv()
        if p in X_LAST:
            whole = out_at(p, qo * QUARTER + xh * EIGHTH, EIGHTH)
            across[p] += (send(whole, whole, xo),)

    def r7(p):
        for copy in across[p]:
            copy.wait_recv()

    state = {}

    def normalize():
        row_sum, square_sum = total_stats(0, stats)
        row_mean = row_sum / D
        row_rstd = lax.rsqrt(square_sum / D - row_mean * row_mean + norm_eps)
        totals[...] = jnp.where(lanes == 0, row_mean, row_rstd)
        centred = (tok_float - row_mean) * row_rstd
        xf[c, slot(0)] = (centred * gain_ref[...][None, :]).astype(BF16)
        start_ring("x", xf.at[c, slot(0)])

    def blk(name, i):
        if name == "f":
            product_rows(hid, branch, i, False)
        else:
            product_rows(ghid, gnorm, i, True)

    def back_step(name, k):
        if name == "f":
            ring_back(name, branch, zf, k)
        else:
            ring_back(name, gnorm, zb, k)

    def finish_out():
        mixed_ref[...] = (
            tok_buf[...].astype(F32) + ring_total("f", branch, zf)
        ).astype(BF16)

    def centred_rows():
        row_mean, row_rstd = totals[:, 0:1], totals[:, 1:2]
        return (tok_buf[...].astype(F32) - row_mean) * row_rstd, row_rstd

    def share_grad():
        grad_scaled = ring_total("b", gnorm, zb) * gain_ref[...][None, :]
        scaled[...] = grad_scaled
        centred, _ = centred_rows()
        state["grad"] = share_stats(
            1,
            jnp.sum(grad_scaled, axis=1, keepdims=True),
            jnp.sum(grad_scaled * centred, axis=1, keepdims=True),
        )

    def finish_grad():
        first_sum, second_sum = total_stats(1, state["grad"])
        centred, row_rstd = centred_rows()
        gin_ref[...] = (
            cf[c, slot(0)].astype(F32)
            + row_rstd * (scaled[...] - first_sum / D - centred * (second_sum / D))
        ).astype(BF16)

    def product(p):
        whole_wait("f" if p < 2 else "b", p % 2)
        weight_product(p)
        r1(2 * p)
        r1(2 * p + 1)

    schedule = (
        (b1, 0, 0), (normalize,), (b1, 0, 1), (f1, 0, 0), (ring_wait, "c", 1), (f1, 0, 1), (b1, 1, 0),
        (ring_wait, "x", 1), (f2, 0, 1), (ring_forward, "x", 1), (f1, 1, 1), (f1, 1, 0), (b1, 1, 1),
        (ring_wait, "x", 2), (ring_forward, "x", 2), (ring_forward, "c", 1), (f2, 0, 0), (f2, 1, 1),
        (f1, 2, 0), (ring_wait, "x", 3), (f1, 2, 1), (ring_forward, "x", 3), (f1, 3, 1), (ring_wait, "c", 2),
        (ring_forward, "c", 2), (f2, 2, 1), (ring_wait, "x", 4), (f1, 3, 0), (f1, 4, 0), (ring_wait, "c", 3),
        (f3, 0, 1), (f1, 4, 1), (ring_forward, "c", 3), (f2, 3, 1), (f2, 4, 1), (f2, 2, 0), (f3, 0, 0),
        (f3, 2, 1), (ring_wait, "c", 4), (f3, 1, 1), (f3, 3, 1), (f2, 3, 0), (f3, 4, 1), (f2, 1, 0),
        (f2, 4, 0), (product, 1), (b1, 4, 0), (f3, 2, 0), (b1, 2, 0), (f3, 3, 0), (f3, 1, 0), (b1, 3, 0),
        (f3, 4, 0), (b2, 0, 0), (product, 0), (blk, "f", 2), (b2, 1, 0), (r2, 0), (blk, "f", 3), (b3, 0, 0),
        (b2, 3, 0), (b2, 2, 0), (r2, 1), (r2, 3), (b3, 1, 0), (b3, 3, 0), (b2, 4, 0), (r3, 0), (b1, 2, 1),
        (r2, 2), (b3, 2, 0), (b1, 4, 1), (b3, 4, 0), (product, 2), (r4, 0), (r3, 1), (back_step, "f", 4),
        (b2, 1, 1), (r2, 5), (b1, 3, 1), (back_step, "f", 3), (blk, "f", 1), (r3, 2), (b2, 2, 1), (r4, 1),
        (b2, 0, 1), (back_step, "f", 2), (b2, 3, 1), (b2, 4, 1), (r5, 0), (r4, 2), (r3, 3), (r5, 1),
        (b3, 0, 1), (b3, 2, 1), (r3, 5), (b3, 3, 1), (b3, 1, 1), (r2, 4), (r5, 2), (b3, 4, 1), (product, 3),
        (blk, "f", 0), (r3, 4), (blk, "b", 3), (r6, 0), (back_step, "f", 1), (blk, "b", 1), (r2, 7),
        (back_step, "b", 4), (r2, 6), (r4, 5), (blk, "b", 0), (blk, "b", 2), (back_step, "b", 3), (r4, 4),
        (r3, 7), (r5, 5), (r3, 6), (r5, 4), (back_step, "b", 2), (r6, 2), (r4, 3), (finish_out,), (r4, 7),
        (r5, 3), (r4, 6), (r6, 1), (r7, 2), (back_step, "b", 1), (r6, 3), (r5, 7), (r6, 5), (r5, 6), (r6, 4),
        (share_grad,), (finish_grad,), (r6, 7), (r7, 3), (r6, 6),
    )
    for step, *where in schedule:
        step(*where)
    for copy in sent:
        copy.wait_send()


def write_out(mixed_in, gin_in, pieces, mixed_ref, gin_ref, gwin_ref, gwout_ref, sems):
    pairs = [(mixed_in, mixed_ref), (gin_in, gin_ref)]
    for p in range(PIECES):
        u, part = p // 2 % 2, p % 2
        if p < PIECES // 2:
            place = pl.ds(part * WIDTH + u * SUB, SUB)
            pairs.append((pieces.at[p], gwout_ref.at[place, :]))
        else:
            for core in range(2):
                place = pl.ds(core * WIDTH + u * SUB, SUB)
                src = pieces.at[p, :, pl.ds(core * SUB, SUB)]
                pairs.append((src, gwin_ref.at[pl.ds(part * HALF, HALF), place]))
    copies = [
        pltpu.make_async_copy(src, dst, sems.at[i]) for i, (src, dst) in enumerate(pairs)
    ]
    for copy in copies:
        copy.start()
    for copy in copies:
        copy.wait()


def shards(tokens, w_in, w_out, gain, cotangent):
    vmem = pl.BlockSpec(memory_space=pltpu.VMEM)
    anywhere = pl.BlockSpec(memory_space=pl.ANY)
    mixed, grad_input, pieces = pl.pallas_call(
        kernel,
        out_shape=(
            pltpu.VMEM((ROWS, WIDTH), BF16),
            pltpu.VMEM((ROWS, WIDTH), BF16),
            pltpu.VMEM((PIECES, HALF, WIDTH), BF16),
        ),
        in_specs=[anywhere, anywhere, anywhere, vmem, anywhere],
        out_specs=(vmem,) * 3,
        scratch_shapes=[
            pltpu.VMEM((2, WIDTH, WIDTH), BF16),
            pltpu.VMEM((2, WIDTH, WIDTH), BF16),
            pltpu.VMEM((2, TOK, WIDTH), BF16),
            pltpu.VMEM((2, TOK, WIDTH), BF16),
            pltpu.VMEM((TOK, WIDTH), BF16),
            pltpu.VMEM((TOK // 2, WIDTH), BF16),
            pltpu.VMEM((TOK, WIDTH), BF16),
            pltpu.VMEM((TOK // 2, WIDTH), BF16),
            pltpu.VMEM((TOK // 2, WIDTH), F32),
            pltpu.VMEM((2, TOK, WIDTH), BF16),
            pltpu.VMEM((2, TOK, WIDTH), BF16),
            pltpu.VMEM((TOK, WIDTH), BF16),
            pltpu.VMEM((TOK, WIDTH), BF16),
            pltpu.VMEM((TOK, WIDTH), BF16),
            pltpu.VMEM((TOK, WIDTH), BF16),
            pltpu.VMEM((2, 8, ROWS), F32),
            pltpu.VMEM((2, 3, 8, ROWS), F32),
            pltpu.VMEM((ROWS, ROWS), F32),
            pltpu.VMEM((ROWS, WIDTH), F32),
            pltpu.VMEM((PIECES, HALF, WIDTH), BF16),
            pltpu.VMEM((PIECES, QUARTER, WIDTH), BF16),
            pltpu.VMEM((PIECES, 2, QUARTER, WIDTH), BF16),
            pltpu.VMEM((PIECES, QUARTER, WIDTH), BF16),
            pltpu.VMEM((PIECES, QUARTER, WIDTH), BF16),
            pltpu.VMEM((ROWS, WIDTH), BF16),
            pltpu.VMEM((WIDTH, 2 * WIDTH), BF16),
            pltpu.VMEM((2 * WIDTH, WIDTH), BF16),
            pltpu.SemaphoreType.DMA((MAX_COPIES,)),
            pltpu.SemaphoreType.DMA((MAX_COPIES,)),
            pltpu.SemaphoreType.DMA((6,)),
        ],
        compiler_params=pltpu.CompilerParams(
            collective_id=0, has_side_effects=True, vmem_limit_bytes=54 << 20
        ),
        cost_estimate=pl.CostEstimate(
            flops=6 * 2 * TOK * WIDTH * 2 * WIDTH, bytes_accessed=12 << 20, transcendentals=0
        ),
        name="mlp_block",
    )(tokens, w_in, w_out, gain, cotangent)
    return pl.pallas_call(
        write_out,
        out_shape=(
            jax.ShapeDtypeStruct((ROWS, WIDTH), BF16),
            jax.ShapeDtypeStruct((ROWS, WIDTH), BF16),
            jax.ShapeDtypeStruct((WIDTH, 2 * WIDTH), BF16),
            jax.ShapeDtypeStruct((2 * WIDTH, WIDTH), BF16),
        ),
        in_specs=[anywhere] * 3,
        out_specs=(anywhere,) * 4,
        scratch_shapes=[pltpu.SemaphoreType.DMA((2 + 3 * PIECES // 2,))],
        compiler_params=pltpu.CompilerParams(vmem_limit_bytes=1 << 20),
        name="write_out",
    )(*(pltpu.with_memory_space_constraint(x, pltpu.VMEM) for x in (mixed, grad_input, pieces)))


def solution(mesh):
    in_specs = (
        P(("dp", "tok"), "hid"),
        P("hid", "tok"),
        P("tok", "hid"),
        P("hid"),
        P(("dp", "tok"), "hid"),
    )
    out_specs = (P(("dp", "tok"), "hid"), P(("dp", "tok"), "hid"), P("hid", "tok"), P("tok", "hid"))
    return jax.shard_map(shards, mesh=mesh, in_specs=in_specs, out_specs=out_specs, check_vma=False)
```

```python
import functools
import math

import jax
import jax.numpy as jnp
from jax import lax
from jax.experimental import pallas as pl
from jax.experimental.pallas import tpu as pltpu
from jax.sharding import PartitionSpec as P

D = 3072
ROWS = 128
WIDTH = 768
TOK = 1024
N_TOK = 8
N_Y = 4
QUARTER = WIDTH // N_Y
EIGHTH = QUARTER // 2
SHARE = ROWS // 2
PIECES = 4
X_LAST = (1,)
MAX_COPIES = 220
SUB = WIDTH // 2
GROUPS = ((0, 128), (128, 256), (384, 256), (640, 256), (896, 128))

norm_eps = 1e-06
GRAD_SCALE = 1.0 / math.sqrt(8192)
MESH = pl.DeviceIdType.MESH
BF16 = jnp.bfloat16
F32 = jnp.float32


def gelu_pair(pre_act):
    cdf_part = 0.5 * (1.0 + lax.erf(pre_act * (1.0 / math.sqrt(2.0))))
    dens_part = jnp.exp(-0.5 * pre_act * pre_act) * (1.0 / math.sqrt(2.0 * math.pi))
    return (pre_act * cdf_part, cdf_part + pre_act * dens_part)


def dot(left_op, right_op):
    return jnp.dot(left_op, right_op, preferred_element_type=F32)


def right_contract(left_op, right_op):
    return lax.dot_general(
        left_op, right_op, (((1,), (1,)), ((), ())), preferred_element_type=F32
    )


def row_contract(left_op, right_op):
    return lax.dot_general(
        left_op, right_op, (((0,), (0,)), ((), ())), preferred_element_type=F32
    )


def block(start, size):
    return pl.ds(start if isinstance(start, int) else pl.multiple_of(start, 16), size)


def kernel(
    tok_ref, win_ref, wout_ref, gain_ref, cot_ref,
    mixed_ref, gin_ref, pieces_ref,
    winc, woutc, xf, cf, pf, rf, pb, rb, slopes, hid, ghid,
    branch, zf, gnorm, zb, stat_out, stat_in, totals, scaled,
    dw, anti, near, qsum, far, tok_buf, win_buf, wout_buf, ssem, rsem, lsem,
):
    dp, z, h = lax.axis_index("dp"), lax.axis_index("tok"), lax.axis_index("hid")
    y, xh = dp // 2, dp % 2
    xl, c = h // 2, h % 2
    zp, zm = (dp, (z + 1) % N_TOK, h), (dp, (z + N_TOK - 1) % N_TOK, h)
    sib = (dp, z, xl * 2 + 1 - c)
    xn = (dp, z, (1 - xl) * 2 + c)
    diag = (dp, z, (1 - xl) * 2 + 1 - c)
    yp, ym = (((y + 1) % N_Y) * 2 + xh, z, h), (((y + N_Y - 1) % N_Y) * 2 + xh, z, h)
    xo = (y * 2 + 1 - xh, z, h)
    peers = (zp, zm, sib, xn, diag, yp, ym, xo)

    own_half, sib_half = c * WIDTH, (1 - c) * WIDTH
    lane_own = pl.ds(pl.multiple_of(own_half, WIDTH), WIDTH)

    barrier = pltpu.get_barrier_semaphore()
    for peer in peers:
        pl.semaphore_signal(barrier, inc=1, device_id=peer, device_id_type=MESH)

    local = [
        pltpu.make_async_copy(tok_ref, tok_buf, lsem.at[0]),
        pltpu.make_async_copy(cot_ref, cf.at[c, pl.ds(0, ROWS)], lsem.at[1]),
        pltpu.make_async_copy(wout_ref.at[lane_own, :], woutc.at[c], lsem.at[2]),
        pltpu.make_async_copy(win_ref.at[:, lane_own], winc.at[c], lsem.at[3]),
        pltpu.make_async_copy(wout_ref, wout_buf, lsem.at[4]),
        pltpu.make_async_copy(win_ref, win_buf, lsem.at[5]),
    ]
    for copy in local:
        copy.start()

    sent = []

    def send(src, dst, peer):
        i = len(sent)
        copy = pltpu.make_async_remote_copy(
            src_ref=src, dst_ref=dst, send_sem=ssem.at[i], recv_sem=rsem.at[i],
            device_id=peer, device_id_type=MESH,
        )
        copy.start()
        sent.append(copy)
        return copy

    def slot(r, lo=0, size=ROWS):
        return block(r * ROWS + lo, size)

    def ring_first(src, buf):
        return [
            (send(src, buf.at[c, slot(1)], zp),),
            (send(src, buf.at[c, slot(2)], zm),),
            send(src, buf.at[c, slot(0)], sib),
        ]

    ring = {"c": {}, "x": {}}
    sib_copies = {"c": {}, "x": {}}
    bufs = {"c": cf, "x": xf}

    def start_ring(name, src):
        up, down, across = ring_first(src, bufs[name])
        ring[name][1] = up + down
        sib_copies[name][0] = across

    def ring_wait(name, k):
        buf = bufs[name]
        for copy in ring[name][k]:
            copy.wait_recv()
        rows = block(*GROUPS[k])
        sib_copies[name][k] = send(buf.at[c, rows], buf.at[c, rows], sib)

    def ring_forward(name, k):
        buf = bufs[name]
        a, b = 2 * k - 1, 2 * k
        if k < 3:
            ring[name][k + 1] = (
                send(buf.at[c, slot(a)], buf.at[c, slot(a + 2)], zp),
                send(buf.at[c, slot(b)], buf.at[c, slot(b + 2)], zm),
            )
        else:
            lo, hi = (0, SHARE), (SHARE, SHARE)
            ring[name][4] = (
                send(buf.at[c, slot(a, *lo)], buf.at[c, slot(7, *lo)], zp),
                send(buf.at[c, slot(b, *hi)], buf.at[c, slot(7, *hi)], zm),
            )

    lanes = lax.broadcasted_iota(jnp.int32, (ROWS, ROWS), 1)

    def share_stats(i, first, second):
        stat_out[i] = jnp.where(lanes == 0, first, second).T[0:8]
        return [
            send(stat_out.at[i], stat_in.at[i, j], peer)
            for j, peer in enumerate((xn, diag, sib))
        ]

    def total_stats(i, copies):
        for copy in copies:
            copy.wait_recv()
        total = (stat_out[i] + stat_in[i, 2]) + (stat_in[i, 0] + stat_in[i, 1])
        columns = jnp.concatenate([total] * (ROWS // 8), axis=0).T
        return columns[:, 0:1], columns[:, 1:2]

    local[0].wait()
    tok_float = tok_buf[...].astype(F32)
    tok_sum = jnp.sum(tok_float, axis=1, keepdims=True)
    tok_squares = jnp.sum(tok_float * tok_float, axis=1, keepdims=True)
    pl.semaphore_wait(barrier, len(peers))
    stats = share_stats(0, tok_sum, tok_squares)
    local[1].wait()
    start_ring("c", cf.at[c, slot(0)])
    weight_copies = {}
    for u in range(2):
        theirs = pl.ds(pl.multiple_of(sib_half + u * SUB, SUB), SUB)
        here = pl.ds(u * SUB, SUB)
        weight_copies["out", u] = send(wout_ref.at[theirs, :], woutc.at[c, here, :], sib)
        weight_copies["in", u] = send(win_ref.at[:, theirs], winc.at[c, :, here], sib)

    def sub(part):
        return pl.ds(part * SUB, SUB)

    arrived = set()

    def arrive(key, *waits):
        if key not in arrived:
            arrived.add(key)
            for wait in waits:
                wait()

    partial_copies = {"f": {}, "b": {}}
    share_copies = {"f": {}, "b": {}}
    whole_copies = {"f": {}, "b": {}}

    def send_partial(name, part, landing, g, u):
        start, count = GROUPS[g]
        half = count // 2
        partial_copies[name][g, u] = send(
            part.at[block(start + (1 - xl) * half, half), sub(u)],
            landing.at[block(start // 2, half), sub(u)],
            xn,
        )

    def send_share(name, buf, g, u):
        start, count = GROUPS[g]
        half = count // 2
        mine = buf.at[c, block(start + xl * half, half), sub(u)]
        share_copies[name][g, u] = send(mine, mine, xn)

    def f1(g, u):
        arrive("win", local[3].wait)
        arrive(("in", u), weight_copies["in", u].wait_recv)
        arrive(("x", g), sib_copies["x"][g].wait_recv)
        rows, cols = block(*GROUPS[g]), sub(u)
        total = dot(xf[0, rows], winc[0, :, cols]) + dot(xf[1, rows], winc[1, :, cols])
        pf[rows, cols] = total.astype(BF16)
        send_partial("f", pf, rf, g, u)

    def b1(g, u):
        arrive("wout", local[2].wait)
        arrive(("out", u), weight_copies["out", u].wait_recv)
        arrive(("c", g), sib_copies["c"][g].wait_recv)
        rows, cols = block(*GROUPS[g]), sub(u)
        total = right_contract(cf[0, rows], woutc[0, cols, :])
        total += right_contract(cf[1, rows], woutc[1, cols, :])
        pb[rows, cols] = total.astype(BF16)
        send_partial("b", pb, rb, g, u)

    def f2(g, u):
        partial_copies["f"][g, u].wait_recv()
        start, count = GROUPS[g]
        mine, landed = start + xl * (count // 2), start // 2

        def tile(n, carry):
            k = n * 32
            pre_act = pf[block(mine + k, 32), sub(u)].astype(F32)
            pre_act += rf[block(landed + k, 32), sub(u)].astype(F32)
            act, slope = gelu_pair(pre_act)
            slopes[block(landed + k, 32), sub(u)] = slope
            hid[c, block(mine + k, 32), sub(u)] = act.astype(BF16)
            return carry

        lax.fori_loop(0, count // 64, tile, 0)
        send_share("f", hid, g, u)

    def b2(g, u):
        partial_copies["b"][g, u].wait_recv()
        start, count = GROUPS[g]
        mine, landed = start + xl * (count // 2), start // 2

        def tile(n, carry):
            k = n * 32
            grad = pb[block(mine + k, 32), sub(u)].astype(F32)
            grad += rb[block(landed + k, 32), sub(u)].astype(F32)
            grad *= slopes[block(landed + k, 32), sub(u)]
            ghid[c, block(mine + k, 32), sub(u)] = grad.astype(BF16)
            return carry

        lax.fori_loop(0, count // 64, tile, 0)
        send_share("b", ghid, g, u)

    def third(name, buf, g, u):
        share_copies[name][g, u].wait_recv()
        whole = buf.at[c, block(*GROUPS[g]), sub(u)]
        whole_copies[name][g, u] = send(whole, whole, sib)

    def f3(g, u):
        third("f", hid, g, u)

    def b3(g, u):
        third("b", ghid, g, u)

    def whole_wait(name, u):
        waits = [whole_copies[name][g, u].wait_recv for g in range(len(GROUPS))]
        arrive((name, "whole", u), *waits)

    def product_rows(src, dst, i, transposed):
        for u in range(2):
            whole_wait("b" if transposed else "f", u)
        rows = block(i * 256, 256)
        if transposed:
            arrive("win_buf", local[5].wait)
            total = right_contract(src[0, rows], win_buf[:, 0:WIDTH])
            total += right_contract(src[1, rows], win_buf[:, WIDTH : 2 * WIDTH])
        else:
            arrive("wout_buf", local[4].wait)
            total = dot(src[0, rows], wout_buf[0:WIDTH, :])
            total += dot(src[1, rows], wout_buf[WIDTH : 2 * WIDTH, :])
        dst[rows, :] = total.astype(BF16)

    def add_rows(dst, at, src, rows, count):
        def tile(n, carry):
            here = block(at + n * 16, 16)
            there = block(rows + n * 16, 16)
            dst[here, :] = (dst[here, :].astype(F32) + src[there, :].astype(F32)).astype(BF16)
            return carry

        lax.fori_loop(0, count // 16, tile, 0)

    back = {"f": {}, "b": {}}

    def ring_back(name, part, landing, k):
        if k == 4:
            back[name][4] = (
                send(part.at[slot(7, 0, SHARE)], landing.at[slot(5, 0, SHARE)], zm),
                send(part.at[slot(7, SHARE, SHARE)], landing.at[slot(6, SHARE, SHARE)], zp),
            )
            return
        a, b = 2 * k - 1, 2 * k
        for copy in back[name][k + 1]:
            copy.wait_recv()
        if k == 3:
            add_rows(part, a * ROWS, landing, a * ROWS, SHARE)
            add_rows(part, b * ROWS + SHARE, landing, b * ROWS + SHARE, SHARE)
        else:
            add_rows(part, a * ROWS, landing, a * ROWS, ROWS)
            add_rows(part, b * ROWS, landing, b * ROWS, ROWS)
        to_a, to_b = (0, 7) if k == 1 else (a - 2, b - 2)
        back[name][k] = (
            send(part.at[slot(a)], landing.at[slot(to_a)], zm),
            send(part.at[slot(b)], landing.at[slot(to_b)], zp),
        )

    def ring_total(name, part, landing):
        for copy in back[name][1]:
            copy.wait_recv()
        total = part[slot(0), :].astype(F32) + landing[slot(0), :].astype(F32)
        return total + landing[slot(7), :].astype(F32)

    qa, qb, qo = (y + 1) % N_Y, (y + N_Y - 1) % N_Y, (y + 2) % N_Y

    def weight_product(p):
        cols = sub(p % 2)
        for core in range(2):
            half = sub(core)
            if p < 2:
                total = row_contract(hid[core, :, cols], cf[c])
                dw[p, half, :] = (total * GRAD_SCALE).astype(BF16)
            else:
                total = row_contract(xf[c], ghid[core, :, cols])
                dw[p, :, half] = (total * GRAD_SCALE).astype(BF16)

    first_hop, second_hop, far_copies, spread, spread_on, across = {}, {}, {}, {}, {}, {}
    low, high = block(0, EIGHTH), block(EIGHTH, EIGHTH)

    def r1(p):
        part = dw.at[p]
        first_hop[p] = (
            send(part.at[block(qo * QUARTER, EIGHTH)], anti.at[p, low], yp),
            send(part.at[block(qo * QUARTER + EIGHTH, EIGHTH)], anti.at[p, high], ym),
        )
        second_hop[p] = (
            send(part.at[block(qa * QUARTER + EIGHTH, EIGHTH)], near.at[p, 0, high], yp),
            send(part.at[block(qb * QUARTER, EIGHTH)], near.at[p, 1, low], ym),
        )

    def r2(p):
        part = dw.at[p]
        for copy in first_hop[p]:
            copy.wait_recv()
        add_rows(part, qa * QUARTER, anti.at[p], 0, EIGHTH)
        add_rows(part, qb * QUARTER + EIGHTH, anti.at[p], EIGHTH, EIGHTH)
        second_hop[p] += (
            send(part.at[block(qa * QUARTER, EIGHTH)], near.at[p, 0, low], yp),
            send(part.at[block(qb * QUARTER + EIGHTH, EIGHTH)], near.at[p, 1, high], ym),
        )

    def r3(p):
        for copy in second_hop[p]:
            copy.wait_recv()

        def tile(n, carry):
            rows = block(n * 16, 16)
            total = dw[p, block(y * QUARTER + n * 16, 16), :].astype(F32)
            total += near[p, 0, rows, :].astype(F32) + near[p, 1, rows, :].astype(F32)
            qsum[p, rows, :] = total.astype(BF16)
            return carry

        lax.fori_loop(0, QUARTER // 16, tile, 0)
        if p in X_LAST:
            theirs = block((1 - xh) * EIGHTH, EIGHTH)
            far_copies[p] = send(qsum.at[p, theirs], far.at[p, low], xo)
        else:
            far_copies[p] = send(qsum.at[p], far.at[p], xo)

    def out_at(p, start, size):
        return pieces_ref.at[p, block(start, size)]

    def r4(p):
        far_copies[p].wait_recv()
        mine, count = (xh * EIGHTH, EIGHTH) if p in X_LAST else (0, QUARTER)

        def tile(n, carry):
            total = qsum[p, block(mine + n * 16, 16), :].astype(F32)
            total += far[p, block(n * 16, 16), :].astype(F32)
            pieces_ref[p, block(y * QUARTER + mine + n * 16, 16), :] = total.astype(BF16)
            return carry

        lax.fori_loop(0, count // 16, tile, 0)
        own = out_at(p, y * QUARTER + mine, count)
        spread[p] = (send(own, own, yp), send(own, own, ym))
        if p in X_LAST:
            across[p] = (send(own, own, xo),)

    def r5(p):
        for copy in spread[p]:
            copy.wait_recv()
        mine, half = (xh * EIGHTH, EIGHTH // 2) if p in X_LAST else (0, EIGHTH)
        behind = out_at(p, qb * QUARTER + mine, half)
        ahead = out_at(p, qa * QUARTER + mine + half, half)
        spread_on[p] = (send(behind, behind, yp), send(ahead, ahead, ym))
        if p in X_LAST:
            for q in (qb, qa):
                whole = out_at(p, q * QUARTER + mine, EIGHTH)
                across[p] += (send(whole, whole, xo),)

    def r6(p):
        for copy in spread_on[p]:
            copy.wait_recv()
        if p in X_LAST:
            whole = out_at(p, qo * QUARTER + xh * EIGHTH, EIGHTH)
            across[p] += (send(whole, whole, xo),)

    def r7(p):
        for copy in across[p]:
            copy.wait_recv()

    state = {}

    def normalize():
        row_sum, square_sum = total_stats(0, stats)
        row_mean = row_sum / D
        row_rstd = lax.rsqrt(square_sum / D - row_mean * row_mean + norm_eps)
        totals[...] = jnp.where(lanes == 0, row_mean, row_rstd)
        centred = (tok_float - row_mean) * row_rstd
        xf[c, slot(0)] = (centred * gain_ref[...][None, :]).astype(BF16)
        start_ring("x", xf.at[c, slot(0)])

    def blk(name, i):
        if name == "f":
            product_rows(hid, branch, i, False)
        else:
            product_rows(ghid, gnorm, i, True)

    def back_step(name, k):
        if name == "f":
            ring_back(name, branch, zf, k)
        else:
            ring_back(name, gnorm, zb, k)

    def finish_out():
        mixed_ref[...] = (
            tok_buf[...].astype(F32) + ring_total("f", branch, zf)
        ).astype(BF16)

    def centred_rows():
        row_mean, row_rstd = totals[:, 0:1], totals[:, 1:2]
        return (tok_buf[...].astype(F32) - row_mean) * row_rstd, row_rstd

    def share_grad():
        grad_scaled = ring_total("b", gnorm, zb) * gain_ref[...][None, :]
        scaled[...] = grad_scaled
        centred, _ = centred_rows()
        state["grad"] = share_stats(
            1,
            jnp.sum(grad_scaled, axis=1, keepdims=True),
            jnp.sum(grad_scaled * centred, axis=1, keepdims=True),
        )

    def finish_grad():
        first_sum, second_sum = total_stats(1, state["grad"])
        centred, row_rstd = centred_rows()
        gin_ref[...] = (
            cf[c, slot(0)].astype(F32)
            + row_rstd * (scaled[...] - first_sum / D - centred * (second_sum / D))
        ).astype(BF16)

    def product(p):
        whole_wait("f" if p < 2 else "b", p % 2)
        weight_product(p)
        r1(p)

    schedule = (
        (normalize,), (b1, 0, 0), (b1, 0, 1), (f1, 0, 0), (ring_wait, "c", 1), (f1, 0, 1), (b1, 1, 0),
        (ring_wait, "x", 1), (ring_forward, "x", 1), (f2, 0, 1), (f1, 1, 1), (b2, 0, 1), (f1, 1, 0),
        (ring_wait, "x", 2), (f2, 0, 0), (ring_forward, "x", 2), (ring_forward, "c", 1), (f1, 2, 0),
        (f1, 2, 1), (f2, 1, 0), (f2, 2, 0), (ring_wait, "x", 3), (ring_forward, "x", 3), (f1, 3, 0),
        (f1, 3, 1), (ring_wait, "c", 2), (ring_forward, "c", 2), (ring_wait, "x", 4), (f3, 2, 0), (f1, 4, 0),
        (f2, 3, 0), (f3, 0, 0), (f1, 4, 1), (ring_wait, "c", 3), (f2, 4, 0), (f2, 1, 1), (f3, 1, 0),
        (ring_forward, "c", 3), (f3, 3, 0), (f2, 2, 1), (f2, 3, 1), (f3, 4, 0), (b2, 0, 0), (f2, 4, 1),
        (ring_wait, "c", 4), (product, 0), (b3, 0, 1), (f3, 0, 1), (b1, 3, 0), (r2, 0), (f3, 4, 1),
        (b1, 2, 0), (f3, 3, 1), (b3, 0, 0), (f3, 2, 1), (b2, 3, 0), (b1, 4, 0), (f3, 1, 1), (product, 1),
        (b2, 1, 0), (blk, "f", 3), (b3, 3, 0), (blk, "f", 1), (b2, 2, 0), (b2, 4, 0), (back_step, "f", 4),
        (blk, "f", 2), (r3, 0), (b3, 1, 0), (b1, 1, 1), (b1, 2, 1), (r2, 1), (b3, 2, 0), (b3, 4, 0),
        (back_step, "f", 3), (product, 2), (r4, 0), (b1, 3, 1), (r2, 2), (b1, 4, 1), (b2, 2, 1), (b2, 3, 1),
        (b3, 2, 1), (b2, 1, 1), (b2, 4, 1), (r3, 1), (r5, 0), (b3, 3, 1), (b3, 1, 1), (b3, 4, 1),
        (product, 3), (r3, 2), (blk, "b", 3), (blk, "b", 2), (back_step, "b", 4), (blk, "f", 0), (r2, 3),
        (r4, 1), (back_step, "f", 2), (blk, "b", 0), (r4, 2), (back_step, "b", 3), (blk, "b", 1), (r6, 0),
        (r3, 3), (back_step, "f", 1), (r5, 1), (back_step, "b", 2), (r4, 3), (r5, 2), (back_step, "b", 1),
        (r6, 1), (r5, 3), (finish_out,), (r6, 2), (r7, 1), (share_grad,), (finish_grad,), (r6, 3),
    )
    for step, *where in schedule:
        step(*where)
    for copy in sent:
        copy.wait_send()


def write_out(mixed_in, gin_in, pieces, mixed_ref, gin_ref, gwin_ref, gwout_ref, sems):
    pairs = [(mixed_in, mixed_ref), (gin_in, gin_ref)]
    for p in range(PIECES):
        for core in range(2):
            half = pl.ds(core * SUB, SUB)
            place = pl.ds(core * WIDTH + (p % 2) * SUB, SUB)
            if p < 2:
                pairs.append((pieces.at[p, half, :], gwout_ref.at[place, :]))
            else:
                pairs.append((pieces.at[p, :, half], gwin_ref.at[:, place]))
    copies = []
    for src, dst in pairs:
        rows = src.shape[0] // 2
        for part in (pl.ds(0, rows), pl.ds(rows, rows)):
            sem = sems.at[len(copies)]
            copies.append(pltpu.make_async_copy(src.at[part, :], dst.at[part, :], sem))
    for copy in copies:
        copy.start()
    for copy in copies:
        copy.wait()


def shards(tokens, w_in, w_out, gain, cotangent):
    vmem = pl.BlockSpec(memory_space=pltpu.VMEM)
    anywhere = pl.BlockSpec(memory_space=pl.ANY)
    mixed, grad_input, pieces = pl.pallas_call(
        kernel,
        out_shape=(
            pltpu.VMEM((ROWS, WIDTH), BF16),
            pltpu.VMEM((ROWS, WIDTH), BF16),
            pltpu.VMEM((PIECES, WIDTH, WIDTH), BF16),
        ),
        in_specs=[anywhere, anywhere, anywhere, vmem, anywhere],
        out_specs=(vmem,) * 3,
        scratch_shapes=[
            pltpu.VMEM((2, WIDTH, WIDTH), BF16),
            pltpu.VMEM((2, WIDTH, WIDTH), BF16),
            pltpu.VMEM((2, TOK, WIDTH), BF16),
            pltpu.VMEM((2, TOK, WIDTH), BF16),
            pltpu.VMEM((TOK, WIDTH), BF16),
            pltpu.VMEM((TOK // 2, WIDTH), BF16),
            pltpu.VMEM((TOK, WIDTH), BF16),
            pltpu.VMEM((TOK // 2, WIDTH), BF16),
            pltpu.VMEM((TOK // 2, WIDTH), F32),
            pltpu.VMEM((2, TOK, WIDTH), BF16),
            pltpu.VMEM((2, TOK, WIDTH), BF16),
            pltpu.VMEM((TOK, WIDTH), BF16),
            pltpu.VMEM((TOK, WIDTH), BF16),
            pltpu.VMEM((TOK, WIDTH), BF16),
            pltpu.VMEM((TOK, WIDTH), BF16),
            pltpu.VMEM((2, 8, ROWS), F32),
            pltpu.VMEM((2, 3, 8, ROWS), F32),
            pltpu.VMEM((ROWS, ROWS), F32),
            pltpu.VMEM((ROWS, WIDTH), F32),
            pltpu.VMEM((PIECES, WIDTH, WIDTH), BF16),
            pltpu.VMEM((PIECES, QUARTER, WIDTH), BF16),
            pltpu.VMEM((PIECES, 2, QUARTER, WIDTH), BF16),
            pltpu.VMEM((PIECES, QUARTER, WIDTH), BF16),
            pltpu.VMEM((PIECES, QUARTER, WIDTH), BF16),
            pltpu.VMEM((ROWS, WIDTH), BF16),
            pltpu.VMEM((WIDTH, 2 * WIDTH), BF16),
            pltpu.VMEM((2 * WIDTH, WIDTH), BF16),
            pltpu.SemaphoreType.DMA((MAX_COPIES,)),
            pltpu.SemaphoreType.DMA((MAX_COPIES,)),
            pltpu.SemaphoreType.DMA((6,)),
        ],
        compiler_params=pltpu.CompilerParams(
            collective_id=0, has_side_effects=True, vmem_limit_bytes=54 << 20
        ),
        cost_estimate=pl.CostEstimate(
            flops=6 * 2 * TOK * WIDTH * 2 * WIDTH, bytes_accessed=12 << 20, transcendentals=0
        ),
        name="mlp_block",
    )(tokens, w_in, w_out, gain, cotangent)
    return pl.pallas_call(
        write_out,
        out_shape=(
            jax.ShapeDtypeStruct((ROWS, WIDTH), BF16),
            jax.ShapeDtypeStruct((ROWS, WIDTH), BF16),
            jax.ShapeDtypeStruct((WIDTH, 2 * WIDTH), BF16),
            jax.ShapeDtypeStruct((2 * WIDTH, WIDTH), BF16),
        ),
        in_specs=[anywhere] * 3,
        out_specs=(anywhere,) * 4,
        scratch_shapes=[pltpu.SemaphoreType.DMA((4 + 4 * PIECES,))],
        compiler_params=pltpu.CompilerParams(vmem_limit_bytes=1 << 20),
        name="write_out",
    )(*(pltpu.with_memory_space_constraint(x, pltpu.VMEM) for x in (mixed, grad_input, pieces)))


def solution(mesh):
    in_specs = (
        P(("dp", "tok"), "hid"),
        P("hid", "tok"),
        P("tok", "hid"),
        P("hid"),
        P(("dp", "tok"), "hid"),
    )
    out_specs = (P(("dp", "tok"), "hid"), P(("dp", "tok"), "hid"), P("hid", "tok"), P("tok", "hid"))
    return jax.shard_map(shards, mesh=mesh, in_specs=in_specs, out_specs=out_specs, check_vma=False)
```
